256 devices in a mesh: expert: 32 (over z, x_lo, core), hidden: 8 (over y, x_hi).
Axes of the slice: x: 4 (x_hi: 2, x_lo: 2; x = x_hi * 2 + x_lo), y: 4, z: 8, core: 2. Of those that a mesh axis runs over, the one named last changes fastest.
Arguments:
- tokens: bfloat16 [768, 7168], P('expert', 'hidden'), may hold values from -6 to 6
- cotangent: bfloat16 [768, 7168], P('expert', 'hidden'), may hold values from -6 to 6
- route_ids: int32 [768, 2], P('expert'), may hold values from 0 to 7, all different within a row; in each aligned block of 24 rows (0 to 23, 24 to 47, ...) at most 10 rows name the same one
- route_gates: float32 [768, 2], P('expert'), may hold values from 0.1 to 0.9
- expert_gate: bfloat16 [8, 4864, 7168], P('hidden', 'expert'), may hold values from -0.0625 to 0.0625
- expert_up: bfloat16 [8, 4864, 7168], P('hidden', 'expert'), may hold values from -0.0625 to 0.0625
- expert_down: bfloat16 [8, 4864, 7168], P('hidden', 'expert'), may hold values from -0.078125 to 0.078125
- dense_gate: bfloat16 [4864, 7168], P('expert', 'hidden'), may hold values from -0.0625 to 0.0625
- dense_up: bfloat16 [4864, 7168], P('expert', 'hidden'), may hold values from -0.0625 to 0.0625
- dense_down: bfloat16 [4864, 7168], P('expert', 'hidden'), may hold values from -0.078125 to 0.078125
Outputs:
- input_grad: bfloat16 [768, 7168], P('expert', 'hidden')
The draws below stay inside these ranges and needn't reach their ends.
Inputs may be any that keep to these rules, and one draw needn't show every extreme that they name: `route_ids`: each row names two different experts. In each aligned block of 24 rows (the tokens of one index of expert) no expert is named by more than 10 rows, a bound that some block reaches.
All inputs are finite; a program needn't handle non-finite values.
Results may differ from the reference program's by a relative error of at most 0.0039.
Values may be sent and summed in bfloat16 or wider, within the bound.
A program may use at most 128 MiB of HBM per device.

```python
import math
from functools import partial
import jax
import jax.numpy as jnp
import numpy as np
from jax import lax

D = 7168
FF_E = 4864
FF_D = 4864
TOK_COL = 24
TOKENS = 768
EXPERTS = 8
CAP = 10
N_EXPERT = 32


def block_levels(key, shape, cuts, low, high):
    factor_of = 1.0
    for position, blocks in cuts:
        heights = jax.random.uniform(jax.random.fold_in(jax.random.fold_in(key, 6), position), (blocks,), jnp.float32, low / len(cuts), high / len(cuts))
        factor_of = factor_of * jnp.repeat(jnp.exp(heights), shape[position] // blocks).reshape((-1,) + (1,) * (len(shape) - 1 - position))
    return factor_of


def deal_out(key, own, number, rows, count, top, limit, lean):
    ranking = jax.random.permutation(key, count)
    crowded, common = portions_of(count, rows * top, limit, lean, True), portions_of(count, rows * top, limit, lean, False)
    places = jnp.arange(count)

    def named(tallies, rotation):
        used = int((tallies > 0).sum())
        fixed = max(1, used // 4)
        moved = fixed + (places - fixed + rotation * (used - fixed)) % max(1, count - fixed)
        return jnp.zeros((count,), jnp.int32).at[ranking[jnp.where(places < fixed, places, moved)]].set(jnp.asarray(tallies, jnp.int32))

    tallies = jnp.where(number % 4 == 0, named(crowded, number // 4), named(common, number - number // 4 - 1))
    mixed = jax.random.permutation(jax.random.fold_in(own, 3), count)
    giver, sink = mixed[0:count // 2 * 2:2], mixed[1:count // 2 * 2:2]
    room = jnp.minimum(tallies[giver] - 1, limit - tallies[sink]) // 2
    room = jnp.where((giver == ranking[0]) | (sink == ranking[0]) | (tallies[sink] == 0), 0, jnp.maximum(room, 0))
    moved = jax.random.randint(jax.random.fold_in(own, 4), (count // 2,), 0, 1 << 20) % (room + 1)
    tallies = tallies.at[giver].add(-moved).at[sink].add(moved)
    members = jnp.searchsorted(jnp.cumsum(tallies), jnp.arange(rows * top), side="right").astype(jnp.int32)
    grid = members.reshape(top, rows).T
    grid = grid[jax.random.permutation(jax.random.fold_in(own, 1), rows)]
    rotation = jax.random.randint(jax.random.fold_in(own, 2), (rows, 1), 0, top)
    return jnp.take_along_axis(grid, (jnp.arange(top)[None, :] + rotation) % top, axis=1)


def portions_of(amount, total, most, skew, full):
    weights = [(1 << 20) // math.isqrt(rank ** skew) + 1 for rank in range(1, amount + 1)]
    largest = most if full else min(most, max(-(-total // amount), total * weights[0] // sum(weights)))
    least = 1 if total - largest >= amount - 1 else 0
    counts, rest = [largest] + [least] * (amount - 1), total - largest - least * (amount - 1)
    while rest > 0:
        free = [i for i in range(1, amount) if counts[i] < largest] or [i for i in range(1, amount) if counts[i] < most]
        whole, remaining = sum([weights[i] for i in free]), rest
        for i in free:
            extra = min(most - counts[i], max(1, remaining * weights[i] // whole), rest)
            counts[i] = counts[i] + extra
            rest = rest - extra
    return np.array(counts)


def normal_values(own_key, dims, scale, bound, shards=(), kind=jnp.bfloat16):
    array = jax.random.normal(own_key, dims, jnp.float32) * scale
    if len(shards) > 0:
        array = block_levels(own_key, dims, shards, -0.22, 0.18) * array
    return jnp.clip(array, min=-bound, max=bound).astype(kind)


def setup_inputs(seed: int = 0) -> dict:
    streams_of = jax.random.split(jax.random.key(seed), 11)
    tokens = normal_values(streams_of[0], (TOKENS, D), 1.0, 6.0, ((0, 32), (1, 8)))
    cotangent = normal_values(streams_of[1], (TOKENS, D), 1.0, 6.0, ((0, 32), (1, 8)))
    route_ids_keys = jax.random.split(jax.random.fold_in(streams_of[2], 1), TOKENS // TOK_COL)
    route_ids_turns = jax.random.permutation(jax.random.fold_in(streams_of[2], 3), TOKENS // TOK_COL)
    route_ids = jax.vmap(lambda own, number: deal_out(jax.random.fold_in(streams_of[2], 2), own, number, TOK_COL, EXPERTS, 2, CAP, 2))(route_ids_keys, route_ids_turns).reshape((TOKENS, 2))
    route_gates = jnp.clip(0.1 + 0.79999997 * jax.random.uniform(streams_of[3], (TOKENS, 2), jnp.float32) ** block_levels(streams_of[3], (TOKENS, 2), ((0, 32),), -0.2, 0.2), 0.1, 0.9)
    expert_gate = normal_values(streams_of[4], (EXPERTS, FF_E, D), D ** -0.5, 0.0625, ((0, 8), (1, 32)))
    expert_up = normal_values(streams_of[5], (EXPERTS, FF_E, D), D ** -0.5, 0.0625, ((0, 8), (1, 32)))
    expert_down = normal_values(streams_of[6], (EXPERTS, FF_E, D), FF_E ** -0.5, 0.078125, ((0, 8), (1, 32)))
    dense_gate = normal_values(streams_of[7], (FF_D, D), D ** -0.5, 0.0625, ((0, 32), (1, 8)))
    dense_up = normal_values(streams_of[8], (FF_D, D), D ** -0.5, 0.0625, ((0, 32), (1, 8)))
    dense_down = normal_values(streams_of[9], (FF_D, D), FF_D ** -0.5, 0.078125, ((0, 32), (1, 8)))
    return dict(tokens=tokens, cotangent=cotangent, route_ids=route_ids, route_gates=route_gates, expert_gate=expert_gate, expert_up=expert_up, expert_down=expert_down, dense_gate=dense_gate, dense_up=dense_up, dense_down=dense_down)


def slot_tables(route_ids, gate_values, experts, capacity):
    count_rows = route_ids.shape[0]
    labels = jnp.arange(experts, dtype=jnp.int32)
    matches = (route_ids[:, :, None] == labels[None, None, :]).astype(jnp.float32)
    flat_hits = matches.reshape(count_rows * 2, experts)
    before = jnp.cumsum(flat_hits, axis=0) - flat_hits
    slot_labels = jnp.arange(capacity).astype(jnp.float32)
    placed = flat_hits[:, :, None] * (before[:, :, None] == slot_labels[None, None, :]).astype(jnp.float32)
    placed = placed.reshape(count_rows, 2, experts, capacity)
    choose = jnp.einsum('tkec->ect', placed)
    weigh = jnp.einsum('tkec,tk->ect', placed, gate_values.astype(jnp.float32), precision=lax.Precision.HIGHEST)
    return choose, weigh


def local_grads(pre_gate, pre_up, upstream):
    sigma_a = jax.nn.sigmoid(pre_gate)
    grad_gate = (upstream * pre_up * sigma_a * (1.0 + pre_gate * (1.0 - sigma_a))).astype(jnp.bfloat16)
    grad_up = (upstream * pre_gate * sigma_a).astype(jnp.bfloat16)
    return grad_gate, grad_up


def expert_terms(rows, cot_rows, w_gate, w_up, w_down):
    pre_gate = jnp.dot(rows, w_gate.T, preferred_element_type=jnp.float32)
    pre_up = jnp.dot(rows, w_up.T, preferred_element_type=jnp.float32)
    upstream = jnp.dot(cot_rows, w_down.T, preferred_element_type=jnp.float32)
    grad_gate, grad_up = local_grads(pre_gate, pre_up, upstream)
    return jnp.dot(grad_gate, w_gate, preferred_element_type=jnp.float32) + jnp.dot(grad_up, w_up, preferred_element_type=jnp.float32)


def reference(tokens, cotangent, route_ids, route_gates, expert_gate, expert_up, expert_down, dense_gate, dense_up, dense_down):
    dense_part = expert_terms(tokens, cotangent, dense_gate, dense_up, dense_down)
    columns = N_EXPERT
    ids_cols = route_ids.reshape(columns, TOK_COL, 2)
    gates_cols = route_gates.reshape(columns, TOK_COL, 2)
    choose, weigh = jax.vmap(partial(slot_tables, experts=EXPERTS, capacity=CAP))(ids_cols, gates_cols)
    token_cols = tokens.reshape(columns, TOK_COL, D).astype(jnp.float32)
    cot_cols = cotangent.reshape(columns, TOK_COL, D).astype(jnp.float32)
    expert_part = jnp.zeros((columns, TOK_COL, D), jnp.float32)
    for expert_no in range(EXPERTS):
        pick = choose[:, expert_no].astype(jnp.float32)
        rows = jnp.einsum('jst,jtd->jsd', pick, token_cols, precision=lax.Precision.HIGHEST)
        rows = rows.reshape(columns * CAP, D).astype(jnp.bfloat16)
        cot_rows = jnp.einsum('jst,jtd->jsd', pick, cot_cols, precision=lax.Precision.HIGHEST)
        cot_rows = cot_rows.reshape(columns * CAP, D).astype(jnp.bfloat16)
        back_rows = expert_terms(rows, cot_rows, expert_gate[expert_no], expert_up[expert_no], expert_down[expert_no])
        expert_part = expert_part + jnp.einsum('jst,jsd->jtd', weigh[:, expert_no], back_rows.reshape(columns, CAP, D), precision=lax.Precision.HIGHEST)
    total = cotangent.astype(jnp.float32) + dense_part + expert_part.reshape(TOKENS, D)
    return total.astype(jnp.bfloat16)
```

```python
import functools

import jax
import jax.numpy as jnp
from jax import lax
from jax.experimental import pallas as pl
from jax.experimental.pallas import tpu as pltpu
from jax.sharding import PartitionSpec as P

MESH = pl.DeviceIdType.MESH
BF, F32 = jnp.bfloat16, jnp.float32
NZ, NH = 8, 8
TOK, PAD = 24, 32
CAP = 10
PIECE = NZ * CAP
NT = (((1,), (1,)), ((), ()))


def grads_of(pre_gate, pre_up, upstream):
    sigma = 1.0 / (1.0 + jnp.exp(-pre_gate))
    grad_gate = upstream * pre_up * sigma * (1.0 + pre_gate * (1.0 - sigma))
    grad_up = upstream * pre_gate * sigma
    return grad_gate.astype(BF), grad_up.astype(BF)


def iota(shape, dim):
    return lax.broadcasted_iota(jnp.int32, shape, dim)


def kernel(
    tok_ref, cot_ref, meta_ref, wg_hbm, wu_hbm, wd_hbm, dg_ref, du_ref, dd_ref, out_ref,
    wg, wu, wd, toks, meta, pick, rows, pre, gg, gu, keep, give, got, chain_out, chain_in, total,
    x_out, x_in, home_out, home_in, dense_w, part_out, part_in, dgrad, res, res_out, res_in,
    w_sem, s1, r1, s3, r3, ring_s, ring_r, x_s, x_r, core_s, core_r, dw_s, dw_r, da_s, da_r, db_s, db_r, dz_s, dz_r,
    ex_s, ex_r, ch_s, ch_r, xx_s, xx_r, hm_s, hm_r,
):
    e, h = lax.axis_index("expert"), lax.axis_index("hidden")
    z, xl, c = e // 4, (e // 2) % 2, e % 2
    feat = tok_ref.shape[1]
    hid = gg.shape[1]

    def at_z(k):
        return lax.rem(z + (k + NZ) % NZ, NZ)

    def dev(zz, xx, cc, hh):
        return (zz * 4 + xx * 2 + cc, hh)

    def ring(k):
        return dev(at_z(k), xl, c, h)

    x_dev, core_dev = dev(z, 1 - xl, c, h), dev(z, xl, 1 - c, h)
    own, oth = c * 2 + xl, c * 2 + 1 - xl

    def remote(src, dst, send, recv, to):
        return pltpu.make_async_remote_copy(
            src_ref=src, dst_ref=dst, send_sem=send, recv_sem=recv, device_id=to, device_id_type=MESH
        )

    sent = []

    def start(*args):
        copy = remote(*args)
        copy.start()
        sent.append(copy)

    def arrived(dst, recv):
        remote(dst, dst, recv, recv, core_dev).wait_recv()

    loads = [
        pltpu.make_async_copy(src.at[0], dst, w_sem.at[i])
        for i, (src, dst) in enumerate(((wg_hbm, wg), (wu_hbm, wu), (wd_hbm, wd)))
    ]
    for load in loads:
        load.start()

    barrier = pltpu.get_barrier_semaphore()

    def greet(to):
        pl.semaphore_signal(barrier, inc=1, device_id=to, device_id_type=MESH)

    for k in range(1, NZ):
        greet(ring(k))
    for k in range(1, NH):
        greet((e, lax.rem(h + k, NH)))
    greet(x_dev)
    greet(core_dev)

    def home_from(k):
        zs = at_z(-k)
        return dev(zs, xl, c, lax.rem(h + zs, NH))

    for k in range(1, NZ):
        greet(home_from(k))

    @pl.when(z != 0)
    def _():
        greet(home_from(0))

    zero = jnp.zeros((PAD - TOK, feat), F32)
    toks[z, 0] = jnp.concatenate([tok_ref[...].astype(F32), zero], 0).astype(BF)
    toks[z, 1] = jnp.concatenate([cot_ref[...].astype(F32), zero], 0).astype(BF)
    lane = iota(meta_ref.shape, 1)
    meta[z] = jnp.where(lane // PAD == z, meta_ref[...], 0.0)
    hpad = dense_w.shape[2]
    zero = jnp.zeros((hpad - hid, feat), F32)
    for k, ref in enumerate((dg_ref, du_ref, dd_ref)):
        dense_w[own, k] = jnp.concatenate([ref[...].astype(F32), zero], 0).astype(BF)

    pl.semaphore_wait(barrier, (NZ - 1) + (NH - 1) + 2 + (NZ - 1) + (z + NZ - 1) // NZ)

    def token_hop(d, step):
        zs = at_z(-d * (step - 1))
        i = (1 - d) // 2
        start(toks.at[zs], toks.at[zs], s1.at[i, step - 1, 0], r1.at[i, step - 1, 0], ring(d))
        start(meta.at[zs], meta.at[zs], s1.at[i, step - 1, 1], r1.at[i, step - 1, 1], ring(d))

    def token_wait(d, step):
        zs = at_z(-d * step)
        i = (1 - d) // 2
        arrived(toks.at[zs], r1.at[i, step - 1, 0])
        arrived(meta.at[zs], r1.at[i, step - 1, 1])

    token_hop(1, 1)
    token_hop(-1, 1)
    start(dense_w.at[own], dense_w.at[own], dw_s.at[0], dw_r.at[0], x_dev)
    start(dense_w.at[own], dense_w.at[own], dw_s.at[1], dw_r.at[1], core_dev)
    for step in range(1, 5):
        token_wait(1, step)
        if step < 4:
            token_hop(1, step + 1)
            token_wait(-1, step)
            if step < 3:
                token_hop(-1, step + 1)

    q = lax.rem(h + z, NH)
    info = meta[0]
    for k in range(1, NZ):
        info = info + meta[k]
    cols = NZ * PAD
    qf = (q + 1).astype(F32)
    match = jnp.where(info[0:1] == qf, 1.0, jnp.where(info[1:2] == qf, 1.0, 0.0))
    a, b = iota((cols, cols), 0), iota((cols, cols), 1)
    before = jnp.where(a // PAD == b // PAD, jnp.where(a < b, 1.0, 0.0), 0.0).astype(BF)
    rank = jnp.dot(jnp.broadcast_to(match, (8, cols)).astype(BF), before, preferred_element_type=F32)[0:1]
    r, t = iota((PIECE, cols), 0), iota((PIECE, cols), 1)
    slot = (r % CAP).astype(F32)
    choose = jnp.where(r // CAP == t // PAD, jnp.where(rank == slot, match, 0.0), 0.0).astype(BF)
    for k in range(2):
        every = toks[:, k].reshape(cols, feat)
        pick[k] = jnp.dot(choose, every, preferred_element_type=F32).astype(BF)

    slice_dev = dev(z, xl, c, q)
    to_plane = remote(pick, rows.at[z, own], s3.at[0], r3.at[0], slice_dev)
    to_self = pltpu.make_async_copy(pick, rows.at[z, own], r3.at[1])

    @pl.when(z != 0)
    def _():
        to_plane.start()
        to_plane.wait()

    @pl.when(z == 0)
    def _():
        to_self.start()
        to_self.wait()

    def zpos(p):
        return at_z(-p) if p <= 4 else at_z(p - 4)

    def core_send(p, kind):
        ref = rows.at[zpos(p), own if kind < 2 else oth, kind % 2]
        start(ref, ref, core_s.at[p, kind], core_r.at[p, kind], core_dev)

    def x_send(p, kind):
        ref = rows.at[zpos(p), own, kind]
        i = p if kind else 8
        start(ref, ref, x_s.at[i], x_r.at[i], x_dev)

    def x_wait(p, kind):
        arrived(rows.at[zpos(p), oth, kind], x_r.at[p if kind else 8])

    def hop_refs(zs):
        return (rows.at[zs, own, 0], rows.at[zs, own, 1], rows.at[zs, oth, 0])

    def hop(d, step, kind):
        ref = hop_refs(at_z(-d * (step - 1)))[kind]
        i = (1 - d) // 2
        start(ref, ref, ring_s.at[i, step - 1, kind], ring_r.at[i, step - 1, kind], ring(d))

    def hop_wait(d, step, kind):
        ref = hop_refs(at_z(-d * step))[kind]
        arrived(ref, ring_r.at[(1 - d) // 2, step - 1, kind])

    x_send(0, 0)
    for kind in range(2):
        hop(1, 1, kind)
        hop(-1, 1, kind)
    x_send(0, 1)
    core_send(0, 0)
    core_send(0, 1)
    x_wait(0, 0)
    hop(1, 1, 2)
    hop(-1, 1, 2)
    core_send(0, 2)

    def forward(step):
        for kind in range(3):
            for d in (1, -1):
                p = step if d == 1 else step + 4
                last = 4 if d == 1 else 3
                if step > last:
                    continue
                hop_wait(d, step, kind)
                if step < last:
                    hop(d, step + 1, kind)
                if kind == 1:
                    x_send(p, 1)
                core_send(p, kind)

    def relay(p):
        x_wait(p, 1)
        core_send(p, 3)

    def multiply(p):
        for kind in range(4):
            rg = (1 - c) * 2 + (xl if kind < 2 else 1 - xl)
            arrived(rows.at[zpos(p), rg, kind % 2], core_r.at[p, kind])

    def accumulate(p, first=False):
        zs = zpos(p)
        col = pl.ds(pl.multiple_of(lax.rem(h - zs + NH, NH) * feat, 128), feat)
        x = rows[zs, :, 0].reshape(4 * PIECE, feat)
        y = rows[zs, :, 1].reshape(4 * PIECE, feat)
        for k, (lhs, w) in enumerate(((x, wg), (x, wu), (y, wd))):
            new = lax.dot_general(lhs, w[:, col], NT, preferred_element_type=F32)
            pre[k] = new if first else pre[k] + new

    arrived(dense_w.at[oth], dw_r.at[0])
    start(dense_w.at[oth], dense_w.at[oth], dw_s.at[2], dw_r.at[2], core_dev)
    arrived(dense_w.at[(1 - c) * 2 + xl], dw_r.at[1])
    arrived(dense_w.at[(1 - c) * 2 + 1 - xl], dw_r.at[2])
    for k in range(3):
        every = toks[:, k // 2].reshape(cols, feat)
        w = dense_w[:, k].reshape(4 * hpad, feat)
        part = lax.dot_general(every, w, NT, preferred_element_type=F32)
        part_out[:, k] = part.astype(BF).reshape(NH, PAD, 4 * hpad)
    for k in range(1, NH):
        hh = lax.rem(h + k, NH)
        start(part_out.at[hh], part_in.at[k], da_s.at[k], da_r.at[k], (e, hh))

    for load in loads:
        load.wait()
    relay(0)
    multiply(0)
    accumulate(0, True)
    forward(1)

    sums = part_out[h].astype(F32)
    for k in range(1, NH):
        arrived(part_in.at[k], da_r.at[k])
        sums = sums + part_in[k].astype(F32)
    dense_gate, dense_up = grads_of(sums[0], sums[1], sums[2])
    dgrad[h, 0] = dense_gate
    dgrad[h, 1] = dense_up
    for k in range(1, NH):
        start(dgrad.at[h], dgrad.at[h], db_s.at[k], db_r.at[k], (e, lax.rem(h + k, NH)))

    for p in (1, 5):
        relay(p)
        multiply(p)
        accumulate(p)
    forward(2)

    for k in range(1, NH):
        arrived(dgrad.at[lax.rem(h + NH - k, NH)], db_r.at[k])
    result = None
    for k in range(2):
        lhs = dgrad[:, k].reshape(cols, 4 * hpad)
        term = jnp.dot(lhs, dense_w[:, k].reshape(4 * hpad, feat), preferred_element_type=F32)
        result = term if result is None else result + term
    result = result.reshape(NZ, PAD, feat)
    res[...] = result
    res_out[...] = result.astype(BF)
    for k in range(1, NZ):
        start(res_out.at[at_z(k)], res_in.at[k], dz_s.at[k], dz_r.at[k], ring(k))

    for p in (2, 6):
        relay(p)
        multiply(p)
        accumulate(p)
    forward(3)
    for p in (3, 7):
        relay(p)
        multiply(p)
        accumulate(p)
    forward(4)
    relay(4)
    multiply(4)
    accumulate(4)

    new_gate, new_up = grads_of(pre[0], pre[1], pre[2])
    gg[...] = new_gate
    gu[...] = new_up

    def slot_z(i):
        odd = i % 2
        return lax.rem(z + odd * (4 - (i + 1) // 2) + (1 - odd) * (4 + i // 2), NZ)

    half = 2 * PIECE

    def produce(i):
        zd = slot_z(i)
        col = pl.ds(pl.multiple_of(lax.rem(h - zd + NH, NH) * feat, 128), feat)

        def rows_of(cc):
            sel = pl.ds(pl.multiple_of(cc * half, half), half)
            return jnp.dot(gg[sel], wg[:, col], preferred_element_type=F32) + jnp.dot(
                gu[sel], wu[:, col], preferred_element_type=F32
            )

        give[i] = rows_of(1 - c).astype(BF).reshape(2, PIECE, feat)
        start(give.at[i], got.at[i], ex_s.at[i], ex_r.at[i], core_dev)
        keep[i] = rows_of(c).reshape(2, PIECE, feat)

    def mine(i, x):
        return keep[i, x] + got[i, x].astype(F32)

    def chain(d, step, x, i):
        k = (1 - d) // 2
        value = mine(i, x)
        if step == 1 and x == k or step > 1:
            arrived(chain_in.at[k, step - 1, x], ch_r.at[k, step - 1, x])
            value = value + chain_in[k, step - 1, x].astype(F32)
        chain_out[k, step, x] = value.astype(BF)
        start(chain_out.at[k, step, x], chain_in.at[k, step, x], ch_s.at[k, step, x], ch_r.at[k, step, x], ring(d))

    def exchanged(i):
        arrived(got.at[i], ex_r.at[i])

    produce(0)
    produce(1)
    exchanged(0)
    chain(1, 0, 0, 0)
    chain(-1, 0, 1, 0)
    produce(2)
    for step in range(1, 4):
        i = 2 * step - 1
        exchanged(i)
        if step == 1:
            chain(1, 1, 1, i)
        produce(i + 2)
        exchanged(i + 1)
        if step == 1:
            chain(-1, 1, 0, i + 1)
            chain(1, 1, 0, i)
            chain(-1, 1, 1, i + 1)
        else:
            for x in (1, 0):
                chain(1, step, x, i)
                chain(-1, step, 1 - x, i + 1)
        if i + 3 < 8:
            produce(i + 3)
    exchanged(7)
    for x in range(2):
        value = mine(7, x)
        for k in range(2):
            arrived(chain_in.at[k, 3, x], ch_r.at[k, 3, x])
            value = value + chain_in[k, 3, x].astype(F32)
        total[x] = value
    x_out[...] = total[1 - xl].astype(BF)
    start(x_out, x_in, xx_s.at[0], xx_r.at[0], x_dev)
    r, t = iota((NZ * 16, PIECE), 0), iota((NZ * 16, PIECE), 1)
    spread = jnp.where(r % 16 < CAP, jnp.where(t == (r // 16) * CAP + r % 16, 1.0, 0.0), 0.0).astype(BF)
    arrived(x_in, xx_r.at[0])
    final = (total[xl] + x_in[...].astype(F32)).astype(BF)
    home_out[...] = jnp.dot(spread, final, preferred_element_type=F32).astype(BF).reshape(NZ, 16, feat)

    back = lax.rem(h - z + NH, NH)
    for k in range(1, NZ):
        zt = at_z(k)
        start(home_out.at[zt], home_in.at[k], hm_s.at[k], hm_r.at[k], dev(zt, xl, c, back))
    home = remote(home_out.at[z], home_in.at[0], hm_s.at[0], hm_r.at[0], dev(z, xl, c, back))
    stay = pltpu.make_async_copy(home_out.at[z], home_in.at[0], hm_r.at[8])

    @pl.when(z != 0)
    def _():
        home.start()

    @pl.when(z == 0)
    def _():
        stay.start()

    n = NZ * 16
    ids0, ids1 = meta_ref[0:1, 0:n], meta_ref[1:2, 0:n]
    g0, g1 = meta_ref[2:3, 0:n], meta_ref[3:4, 0:n]
    r, t = iota((n, n), 0), iota((n, n), 1)
    label = ((h + (z - r // 16 + NZ) % NZ) % NH + 1).astype(F32)
    hit0, hit1 = jnp.where(ids0 == label, 1.0, 0.0), jnp.where(ids1 == label, 1.0, 0.0)
    before = jnp.where(r // PAD == t // PAD, jnp.where(r < t, 1.0, 0.0), 0.0).astype(BF)
    rank = jnp.dot((hit0 + hit1).astype(BF), before, preferred_element_type=F32)
    weigh = jnp.where(rank == (r % 16).astype(F32), hit0 * g0 + hit1 * g1, 0.0)

    dense = res[z]
    for k in range(1, NZ):
        arrived(res_in.at[k], dz_r.at[k])
        dense = dense + res_in[k].astype(F32)

    for k in range(1, NZ):
        arrived(home_in.at[k], hm_r.at[k])

    @pl.when(z != 0)
    def _():
        home.wait()

    @pl.when(z == 0)
    def _():
        stay.wait()

    expert = lax.dot_general(
        weigh, home_in[...].reshape(n, feat).astype(F32), (((0,), (0,)), ((), ())),
        precision=lax.Precision.HIGHEST, preferred_element_type=F32,
    )
    out_ref[...] = (cot_ref[...].astype(F32) + dense[0:TOK] + expert[0:TOK]).astype(BF)

    for copy in sent:
        copy.wait_send()


def on_device(tokens, cotangent, route_ids, route_gates, expert_gate, expert_up, expert_down, dense_gate, dense_up, dense_down):
    feat = tokens.shape[1]
    hid, width = expert_gate.shape[1], expert_gate.shape[2]
    hpad = (hid + 15) // 16 * 16
    meta = jnp.concatenate([route_ids.astype(F32) + 1.0, route_gates], axis=1).T
    meta = jnp.tile(jnp.pad(meta, ((0, 4), (0, PAD - TOK))), (1, NZ))
    dma, vmem = pltpu.SemaphoreType.DMA, pltpu.VMEM
    scratch = [
        vmem((hid, width), BF), vmem((hid, width), BF), vmem((hid, width), BF),
        vmem((NZ, 2, PAD, feat), BF),
        vmem((NZ, 8, NZ * PAD), F32),
        vmem((2, PIECE, feat), BF),
        vmem((NZ, 4, 2, PIECE, feat), BF),
        vmem((3, 4 * PIECE, hid), F32),
        vmem((4 * PIECE, hid), BF), vmem((4 * PIECE, hid), BF),
        vmem((NZ, 2, PIECE, feat), F32),
        vmem((NZ, 2, PIECE, feat), BF), vmem((NZ, 2, PIECE, feat), BF),
        vmem((2, 4, 2, PIECE, feat), BF), vmem((2, 4, 2, PIECE, feat), BF),
        vmem((2, PIECE, feat), F32),
        vmem((PIECE, feat), BF), vmem((PIECE, feat), BF),
        vmem((NZ, 16, feat), BF), vmem((NZ, 16, feat), BF),
        vmem((4, 3, hpad, feat), BF),
        vmem((NH, 3, PAD, 4 * hpad), BF), vmem((NH, 3, PAD, 4 * hpad), BF),
        vmem((NH, 2, PAD, 4 * hpad), BF),
        vmem((NZ, PAD, feat), F32), vmem((NZ, PAD, feat), BF), vmem((NZ, PAD, feat), BF),
        dma((3,)), dma((2, 4, 2)), dma((2, 4, 2)), dma((2,)), dma((2,)),
        dma((2, 4, 3)), dma((2, 4, 3)), dma((9,)), dma((9,)), dma((8, 4)), dma((8, 4)),
        dma((3,)), dma((3,)), dma((8,)), dma((8,)), dma((8,)), dma((8,)), dma((8,)), dma((8,)),
        dma((8,)), dma((8,)), dma((2, 4, 2)), dma((2, 4, 2)), dma((1,)), dma((1,)), dma((9,)), dma((9,)),
    ]
    whole, far = pl.BlockSpec(memory_space=pltpu.VMEM), pl.BlockSpec(memory_space=pl.ANY)
    return pl.pallas_call(
        kernel,
        out_shape=jax.ShapeDtypeStruct(tokens.shape, BF),
        in_specs=[whole] * 3 + [far] * 3 + [whole] * 3,
        out_specs=whole,
        scratch_shapes=scratch,
        compiler_params=pltpu.CompilerParams(collective_id=0, has_side_effects=True, vmem_limit_bytes=56 << 20),
        name="layer",
    )(tokens, cotangent, meta, expert_gate, expert_up, expert_down, dense_gate, dense_up, dense_down)


def solution(mesh):
    in_specs = (
        P("expert", "hidden"),
        P("expert", "hidden"),
        P("expert", None),
        P("expert", None),
        P("hidden", "expert", None),
        P("hidden", "expert", None),
        P("hidden", "expert", None),
        P("expert", "hidden"),
        P("expert", "hidden"),
        P("expert", "hidden"),
    )
    return jax.shard_map(on_device, mesh=mesh, in_specs=in_specs, out_specs=P("expert", "hidden"), check_vma=False)
```

```python
import functools

import jax
import jax.numpy as jnp
from jax import lax
from jax.experimental import pallas as pl
from jax.experimental.pallas import tpu as pltpu
from jax.sharding import PartitionSpec as P

MESH = pl.DeviceIdType.MESH
BF, F32 = jnp.bfloat16, jnp.float32
NZ, NH = 8, 8
TOK, PAD = 24, 32
BLOCK = 2 * TOK
CAP = 10
PIECE = NZ * CAP
NT = (((1,), (1,)), ((), ()))


def grads_of(pre_gate, pre_up, upstream):
    sigma = 1.0 / (1.0 + jnp.exp(-pre_gate))
    grad_gate = upstream * pre_up * sigma * (1.0 + pre_gate * (1.0 - sigma))
    grad_up = upstream * pre_gate * sigma
    return grad_gate.astype(BF), grad_up.astype(BF)


def iota(shape, dim):
    return lax.broadcasted_iota(jnp.int32, shape, dim)


def kernel(
    tok_ref, cot_ref, meta_ref, wg_hbm, wu_hbm, wd_hbm, dg_ref, du_ref, dd_ref, out_ref,
    wg, wu, wd, toks, meta, pick, rows, pre, gg, gu, keep, give, got, chain_out, chain_in, total,
    x_out, x_in, home_out, home_in, dense_w, part_out, part_in, dgrad, res, res_x_out, res_x_in, res_out, res_in,
    w_sem, s1, r1, s3, r3, ring_s, ring_r, x_s, x_r, core_s, core_r, dw_s, dw_r, da_s, da_r, db_s, db_r, dz_s, dz_r,
    ex_s, ex_r, ch_s, ch_r, xx_s, xx_r, hm_s, hm_r,
):
    e, h = lax.axis_index("expert"), lax.axis_index("hidden")
    z, xl, c = e // 4, (e // 2) % 2, e % 2
    feat = tok_ref.shape[1]
    hid = gg.shape[1]

    def at_z(k):
        return lax.rem(z + (k + NZ) % NZ, NZ)

    def dev(zz, xx, cc, hh):
        return (zz * 4 + xx * 2 + cc, hh)

    def ring(k):
        return dev(at_z(k), xl, c, h)

    x_dev, core_dev = dev(z, 1 - xl, c, h), dev(z, xl, 1 - c, h)

    def remote(src, dst, send, recv, to):
        return pltpu.make_async_remote_copy(
            src_ref=src, dst_ref=dst, send_sem=send, recv_sem=recv, device_id=to, device_id_type=MESH
        )

    sent = []

    def start(*args):
        copy = remote(*args)
        copy.start()
        sent.append(copy)

    def arrived(dst, recv):
        remote(dst, dst, recv, recv, core_dev).wait_recv()

    loads = [
        pltpu.make_async_copy(src.at[0], dst, w_sem.at[i])
        for i, (src, dst) in enumerate(((wg_hbm, wg), (wu_hbm, wu), (wd_hbm, wd)))
    ]
    for load in loads:
        load.start()

    barrier = pltpu.get_barrier_semaphore()

    def greet(to):
        pl.semaphore_signal(barrier, inc=1, device_id=to, device_id_type=MESH)

    for k in range(1, NZ):
        greet(ring(k))
    for k in range(1, NH):
        greet((e, lax.rem(h + k, NH)))
    greet(x_dev)
    greet(core_dev)

    def home_from(k):
        zs = at_z(-k)
        return dev(zs, xl, c, lax.rem(h + zs, NH))

    for k in range(1, NZ):
        greet(home_from(k))

    @pl.when(z != 0)
    def _():
        greet(home_from(0))

    toks[xl, z] = jnp.concatenate([tok_ref[...].astype(F32), cot_ref[...].astype(F32)], 0).astype(BF)
    lane = iota(meta_ref.shape, 1)
    meta[xl, z] = jnp.where(lane // BLOCK == z, meta_ref[...], 0.0)
    hpad = dense_w.shape[2]
    zero = jnp.zeros((hpad - hid, feat), F32)
    for k, ref in enumerate((dg_ref, du_ref, dd_ref)):
        dense_w[k, c] = jnp.concatenate([ref[...].astype(F32), zero], 0).astype(BF)

    pl.semaphore_wait(barrier, (NZ - 1) + (NH - 1) + 2 + (NZ - 1) + (z + NZ - 1) // NZ)

    def zpos(p):
        return at_z(-p) if p <= 4 else at_z(p - 4)

    def token_hop(d, step):
        zs = at_z(-d * (step - 1))
        i = (1 - d) // 2
        start(toks.at[xl, zs], toks.at[xl, zs], s1.at[i, step - 1, 0], r1.at[i, step - 1, 0], ring(d))
        start(meta.at[xl, zs], meta.at[xl, zs], s1.at[i, step - 1, 1], r1.at[i, step - 1, 1], ring(d))

    def token_wait(d, step):
        zs = at_z(-d * step)
        i = (1 - d) // 2
        arrived(toks.at[xl, zs], r1.at[i, step - 1, 0])
        arrived(meta.at[xl, zs], r1.at[i, step - 1, 1])

    def token_x(p):
        zs = zpos(p)
        start(toks.at[xl, zs], toks.at[xl, zs], x_s.at[p, 0], x_r.at[p, 0], x_dev)
        start(meta.at[xl, zs], meta.at[xl, zs], x_s.at[p, 1], x_r.at[p, 1], x_dev)

    token_hop(1, 1)
    token_hop(-1, 1)
    token_x(0)
    for k in range(3):
        start(dense_w.at[k, c], dense_w.at[k, c], dw_s.at[k], dw_r.at[k], core_dev)
    for step in range(1, 5):
        token_wait(1, step)
        if step < 4:
            token_hop(1, step + 1)
        token_x(step)
        if step < 4:
            token_wait(-1, step)
            if step < 3:
                token_hop(-1, step + 1)
            token_x(step + 4)
    for p in range(NZ):
        zs = zpos(p)
        arrived(toks.at[1 - xl, zs], x_r.at[p, 0])
        arrived(meta.at[1 - xl, zs], x_r.at[p, 1])

    y, xh = h // 2, h % 2

    def plane(dy, flip):
        return lax.rem(y + dy + 8, 4) * 2 + (1 - xh if flip else xh)

    targets = (plane(-z, True), plane(2, False), plane(1, False), plane(-1, False), h)
    cols = NZ * BLOCK
    row = iota((8, cols), 0)
    label = jnp.full((8, cols), -1, jnp.int32)
    for i, q in enumerate(targets):
        label = jnp.where(row == i, q + 1, label)
    label = label.astype(F32)
    a, b = iota((cols, cols), 0), iota((cols, cols), 1)
    before = jnp.where(a // TOK == b // TOK, jnp.where(a < b, 1.0, 0.0), 0.0).astype(BF)
    matches, ranks = [], []
    for x in range(2):
        info = meta[x, 0]
        for k in range(1, NZ):
            info = info + meta[x, k]
        match = jnp.where(info[0:1] == label, 1.0, jnp.where(info[1:2] == label, 1.0, 0.0))
        matches.append(match)
        ranks.append(jnp.dot(match.astype(BF), before, preferred_element_type=F32))
    r, t = iota((2 * PIECE, cols), 0), iota((2 * PIECE, cols), 1)
    slot = (r % CAP).astype(F32)
    inside = t // TOK == (r % PIECE) // CAP * 2 + r // PIECE

    def chosen(i, x):
        choose = jnp.where(inside, jnp.where(ranks[x][i : i + 1] == slot, matches[x][i : i + 1], 0.0), 0.0)
        every = toks[x].reshape(cols, feat)
        both = jnp.dot(choose.astype(BF), every, preferred_element_type=F32).astype(BF)
        return both.reshape(2, PIECE, feat)

    for i in range(4):
        for x in range(2):
            both = chosen(i, x)
            for k in range(2):
                pick[i, k, x] = both[k]
        for k in range(4):
            start(
                pick.at[i, k // 2, k % 2], rows.at[h, c, k // 2, k % 2], s3.at[i, k], r3.at[i, k],
                (e, targets[i]),
            )
    for x in range(2):
        both = chosen(4, x)
        for k in range(2):
            rows[h, c, k, x] = both[k]

    slices = (h, plane(-2, False), plane(-1, False), plane(1, False), plane(z, True), plane(z - 1, True), plane(z + 1, True), plane(z + 2, True))

    def chunk(p, k):
        return rows.at[slices[p], c, k // 2, k % 2]

    def core_send(p, k):
        start(chunk(p, k), chunk(p, k), core_s.at[p, k], core_r.at[p, k], core_dev)

    def hop(d, step, k):
        ref = chunk(4 if step == 0 else (5 if d == 1 else 6), k)
        i = (1 - d) // 2
        start(ref, ref, ring_s.at[i, step, k], ring_r.at[i, step, k], ring(d))

    def multiply(p):
        for k in range(4):
            arrived(rows.at[slices[p], 1 - c, k // 2, k % 2], core_r.at[p, k])

    def accumulate(p, first=False):
        multiply(p)
        sl = slices[p]
        col = pl.ds(pl.multiple_of(sl * feat, 128), feat)
        x = rows[sl, :, 0].reshape(4 * PIECE, feat)
        y = rows[sl, :, 1].reshape(4 * PIECE, feat)
        for k, (lhs, w) in enumerate(((x, wg), (x, wu), (y, wd))):
            new = lax.dot_general(lhs, w[:, col], NT, preferred_element_type=F32)
            pre[k] = new if first else pre[k] + new

    for k in range(4):
        core_send(0, k)

    for k in range(3):
        arrived(dense_w.at[k, 1 - c], dw_r.at[k])
    every = toks[...].reshape(2 * cols, feat)
    for k in range(3):
        w = dense_w[k].reshape(2 * hpad, feat)
        part = lax.dot_general(every, w, NT, preferred_element_type=F32).reshape(2, NZ, BLOCK, 2 * hpad)
        part = part[:, :, 0:TOK] if k < 2 else part[:, :, TOK:BLOCK]
        for hh in range(NH):
            part_out[hh, k] = jnp.concatenate([part[0, hh], part[1, hh]], 0).astype(BF)
    for k in range(1, NH):
        hh = lax.rem(h + k, NH)
        start(part_out.at[hh], part_in.at[k], da_s.at[k], da_r.at[k], (e, hh))

    for k in range(4):
        arrived(chunk(4, k), r3.at[0, k])
        hop(1, 0, k)
        hop(-1, 0, k)
        core_send(4, k)

    for load in loads:
        load.wait()
    accumulate(0, True)

    for i in (2, 3):
        for k in range(4):
            arrived(chunk(i, k), r3.at[i, k])
            core_send(i, k)
    for k in range(4):
        for d in (1, -1):
            arrived(chunk(5 if d == 1 else 6, k), ring_r.at[(1 - d) // 2, 0, k])
            if (k < 2) == (d == 1):
                hop(d, 1, k)
            core_send(5 if d == 1 else 6, k)
    accumulate(4)
    accumulate(2)
    accumulate(3)
    for k in range(4):
        arrived(chunk(1, k), r3.at[1, k])
        core_send(1, k)
    for k in range(4):
        arrived(chunk(7, k), ring_r.at[k // 2, 1, k])
        core_send(7, k)
    accumulate(5)
    accumulate(6)
    accumulate(1)

    sums = part_out[h].astype(F32)
    for k in range(1, NH):
        arrived(part_in.at[k], da_r.at[k])
        sums = sums + part_in[k].astype(F32)
    dense_gate, dense_up = grads_of(sums[0], sums[1], sums[2])
    dgrad[0, h] = dense_gate
    dgrad[1, h] = dense_up
    for k in range(1, NH):
        start(dgrad.at[:, h], dgrad.at[:, h], db_s.at[k], db_r.at[k], (e, lax.rem(h + k, NH)))

    accumulate(7)

    def dense_result():
        for k in range(1, NH):
            arrived(dgrad.at[:, lax.rem(h + NH - k, NH)], db_r.at[k])
        result = None
        for k in range(2):
            lhs = dgrad[k].reshape(cols, 2 * hpad)
            term = jnp.dot(lhs, dense_w[k].reshape(2 * hpad, feat), preferred_element_type=F32)
            result = term if result is None else result + term
        result = result.reshape(NZ, 2, TOK, feat)
        for x in range(2):
            res[x] = result[:, x]
        res_x_out[...] = res[1 - xl].reshape(NZ * TOK, feat).astype(BF)
        start(res_x_out, res_x_in, xx_s.at[1], xx_r.at[1], x_dev)

    def dense_reduce():
        arrived(res_x_in, xx_r.at[1])
        result = res[xl] + res_x_in[...].astype(F32).reshape(NZ, TOK, feat)
        res[xl] = result
        zero = jnp.zeros((PAD - TOK, feat), F32)
        for k in range(NZ):
            res_out[k] = jnp.concatenate([result[k], zero], 0).astype(BF)
        for k in range(1, NZ):
            start(res_out.at[at_z(k)], res_in.at[k], dz_s.at[k], dz_r.at[k], ring(k))

    new_gate, new_up = grads_of(pre[0], pre[1], pre[2])
    gg[...] = new_gate
    gu[...] = new_up

    def slot_z(i):
        odd = i % 2
        return lax.rem(z + odd * (4 - (i + 1) // 2) + (1 - odd) * (4 + i // 2), NZ)

    half = 2 * PIECE

    def produce(i):
        zd = slot_z(i)
        col = pl.ds(pl.multiple_of(lax.rem(h - zd + NH, NH) * feat, 128), feat)

        def rows_of(cc):
            sel = pl.ds(pl.multiple_of(cc * half, half), half)
            return jnp.dot(gg[sel], wg[:, col], preferred_element_type=F32) + jnp.dot(
                gu[sel], wu[:, col], preferred_element_type=F32
            )

        give[i] = rows_of(1 - c).astype(BF).reshape(2, PIECE, feat)
        start(give.at[i], got.at[i], ex_s.at[i], ex_r.at[i], core_dev)
        keep[i] = rows_of(c).reshape(2, PIECE, feat)

    def mine(i, x):
        return keep[i, x] + got[i, x].astype(F32)

    def chain(d, step, x, i):
        k = (1 - d) // 2
        value = mine(i, x)
        if step == 1 and x == k or step > 1:
            arrived(chain_in.at[k, step - 1, x], ch_r.at[k, step - 1, x])
            value = value + chain_in[k, step - 1, x].astype(F32)
        chain_out[k, step, x] = value.astype(BF)
        start(chain_out.at[k, step, x], chain_in.at[k, step, x], ch_s.at[k, step, x], ch_r.at[k, step, x], ring(d))

    def exchanged(i):
        arrived(got.at[i], ex_r.at[i])

    produce(0)
    produce(1)
    exchanged(0)
    chain(1, 0, 0, 0)
    chain(-1, 0, 1, 0)
    produce(2)
    for step in range(1, 4):
        i = 2 * step - 1
        exchanged(i)
        if step == 1:
            chain(1, 1, 1, i)
        produce(i + 2)
        exchanged(i + 1)
        if step == 1:
            chain(-1, 1, 0, i + 1)
            chain(1, 1, 0, i)
            chain(-1, 1, 1, i + 1)
        else:
            for x in (1, 0):
                chain(1, step, x, i)
                chain(-1, step, 1 - x, i + 1)
        if i + 3 < 8:
            produce(i + 3)
        if step == 2:
            dense_result()
        if step == 3:
            dense_reduce()
    exchanged(7)
    for x in range(2):
        value = mine(7, x)
        for k in range(2):
            arrived(chain_in.at[k, 3, x], ch_r.at[k, 3, x])
            value = value + chain_in[k, 3, x].astype(F32)
        total[x] = value
    x_out[...] = total[1 - xl].astype(BF)
    start(x_out, x_in, xx_s.at[0], xx_r.at[0], x_dev)
    r, t = iota((NZ * 16, PIECE), 0), iota((NZ * 16, PIECE), 1)
    spread = jnp.where(r % 16 < CAP, jnp.where(t == (r // 16) * CAP + r % 16, 1.0, 0.0), 0.0).astype(BF)
    arrived(x_in, xx_r.at[0])
    final = (total[xl] + x_in[...].astype(F32)).astype(BF)
    home_out[...] = jnp.dot(spread, final, preferred_element_type=F32).astype(BF).reshape(NZ, 16, feat)

    back = lax.rem(h - z + NH, NH)
    for k in range(1, NZ):
        zt = at_z(k)
        start(home_out.at[zt], home_in.at[k], hm_s.at[k], hm_r.at[k], dev(zt, xl, c, back))
    home = remote(home_out.at[z], home_in.at[0], hm_s.at[0], hm_r.at[0], dev(z, xl, c, back))
    stay = pltpu.make_async_copy(home_out.at[z], home_in.at[0], hm_r.at[8])

    @pl.when(z != 0)
    def _():
        home.start()

    @pl.when(z == 0)
    def _():
        stay.start()

    n = NZ * 16
    ids0, ids1 = meta_ref[0:1, 0:n], meta_ref[1:2, 0:n]
    g0, g1 = meta_ref[2:3, 0:n], meta_ref[3:4, 0:n]
    r, t = iota((n, n), 0), iota((n, n), 1)
    label = ((h + (z - r // 16 + NZ) % NZ) % NH + 1).astype(F32)
    hit0, hit1 = jnp.where(ids0 == label, 1.0, 0.0), jnp.where(ids1 == label, 1.0, 0.0)
    before = jnp.where(r // TOK == t // TOK, jnp.where(r < t, 1.0, 0.0), 0.0).astype(BF)
    rank = jnp.dot((hit0 + hit1).astype(BF), before, preferred_element_type=F32)
    weigh = jnp.where(rank == (r % 16).astype(F32), hit0 * g0 + hit1 * g1, 0.0)

    dense = res[xl, z]
    for k in range(1, NZ):
        arrived(res_in.at[k], dz_r.at[k])
        dense = dense + res_in[k, 0:TOK].astype(F32)

    for k in range(1, NZ):
        arrived(home_in.at[k], hm_r.at[k])

    @pl.when(z != 0)
    def _():
        home.wait()

    @pl.when(z == 0)
    def _():
        stay.wait()

    expert = lax.dot_general(
        weigh, home_in[...].reshape(n, feat).astype(F32), (((0,), (0,)), ((), ())),
        precision=lax.Precision.HIGHEST, preferred_element_type=F32,
    )
    out_ref[...] = (cot_ref[...].astype(F32) + dense + expert[0:TOK]).astype(BF)

    for copy in sent:
        copy.wait_send()


def on_device(tokens, cotangent, route_ids, route_gates, expert_gate, expert_up, expert_down, dense_gate, dense_up, dense_down):
    feat = tokens.shape[1]
    hid, width = expert_gate.shape[1], expert_gate.shape[2]
    hpad = (hid + 15) // 16 * 16
    meta = jnp.concatenate([route_ids.astype(F32) + 1.0, route_gates], axis=1).T
    meta = jnp.tile(jnp.pad(meta, ((0, 4), (0, 0))), (1, 2 * NZ))
    dma, vmem = pltpu.SemaphoreType.DMA, pltpu.VMEM
    scratch = [
        vmem((hid, width), BF), vmem((hid, width), BF), vmem((hid, width), BF),
        vmem((2, NZ, BLOCK, feat), BF),
        vmem((2, NZ, 8, NZ * BLOCK), F32),
        vmem((4, 2, 2, PIECE, feat), BF),
        vmem((NH, 2, 2, 2, PIECE, feat), BF),
        vmem((3, 4 * PIECE, hid), F32),
        vmem((4 * PIECE, hid), BF), vmem((4 * PIECE, hid), BF),
        vmem((NZ, 2, PIECE, feat), F32),
        vmem((NZ, 2, PIECE, feat), BF), vmem((NZ, 2, PIECE, feat), BF),
        vmem((2, 4, 2, PIECE, feat), BF), vmem((2, 4, 2, PIECE, feat), BF),
        vmem((2, PIECE, feat), F32),
        vmem((PIECE, feat), BF), vmem((PIECE, feat), BF),
        vmem((NZ, 16, feat), BF), vmem((NZ, 16, feat), BF),
        vmem((3, 2, hpad, feat), BF),
        vmem((NH, 3, BLOCK, 2 * hpad), BF), vmem((NH, 3, BLOCK, 2 * hpad), BF),
        vmem((2, NH, BLOCK, 2 * hpad), BF),
        vmem((2, NZ, TOK, feat), F32),
        vmem((NZ * TOK, feat), BF), vmem((NZ * TOK, feat), BF),
        vmem((NZ, PAD, feat), BF), vmem((NZ, PAD, feat), BF),
        dma((3,)), dma((2, 4, 2)), dma((2, 4, 2)), dma((4, 4)), dma((4, 4)),
        dma((2, 2, 4)), dma((2, 2, 4)), dma((8, 2)), dma((8, 2)), dma((8, 4)), dma((8, 4)),
        dma((3,)), dma((3,)), dma((8,)), dma((8,)), dma((8,)), dma((8,)), dma((8,)), dma((8,)),
        dma((8,)), dma((8,)), dma((2, 4, 2)), dma((2, 4, 2)), dma((2,)), dma((2,)), dma((9,)), dma((9,)),
    ]
    whole, far = pl.BlockSpec(memory_space=pltpu.VMEM), pl.BlockSpec(memory_space=pl.ANY)
    return pl.pallas_call(
        kernel,
        out_shape=jax.ShapeDtypeStruct(tokens.shape, BF),
        in_specs=[whole] * 3 + [far] * 3 + [whole] * 3,
        out_specs=whole,
        scratch_shapes=scratch,
        compiler_params=pltpu.CompilerParams(collective_id=0, has_side_effects=True, vmem_limit_bytes=56 << 20),
        name="layer",
    )(tokens, cotangent, meta, expert_gate, expert_up, expert_down, dense_gate, dense_up, dense_down)


def solution(mesh):
    in_specs = (
        P("expert", "hidden"),
        P("expert", "hidden"),
        P("expert", None),
        P("expert", None),
        P("hidden", "expert", None),
        P("hidden", "expert", None),
        P("hidden", "expert", None),
        P("expert", "hidden"),
        P("expert", "hidden"),
        P("expert", "hidden"),
    )
    return jax.shard_map(on_device, mesh=mesh, in_specs=in_specs, out_specs=P("expert", "hidden"), check_vma=False)
```

```python
import functools

import jax
import jax.numpy as jnp
from jax import lax
from jax.experimental import pallas as pl
from jax.experimental.pallas import tpu as pltpu
from jax.sharding import PartitionSpec as P

MESH = pl.DeviceIdType.MESH
BF, F32 = jnp.bfloat16, jnp.float32
NZ, NH = 8, 8
TOK, PAD = 24, 32
BLOCK = 2 * TOK
CAP = 10
PIECE = NZ * CAP
NT = (((1,), (1,)), ((), ()))


def grads_of(pre_gate, pre_up, upstream):
    sigma = 1.0 / (1.0 + jnp.exp(-pre_gate))
    grad_gate = upstream * pre_up * sigma * (1.0 + pre_gate * (1.0 - sigma))
    grad_up = upstream * pre_gate * sigma
    return grad_gate.astype(BF), grad_up.astype(BF)


def iota(shape, dim):
    return lax.broadcasted_iota(jnp.int32, shape, dim)


def kernel(
    tok_ref, cot_ref, ids_ref, gates_ref, wg_hbm, wu_hbm, wd_hbm, dg_ref, du_ref, dd_ref, out_ref,
    wg, wu, wd, toks, meta, pick, rows, pre, gg, gu, keep, give, got, chain_out, chain_in, total,
    x_out, x_in, home_out, home_in, dense_w, part_out, part_in, dgrad, res, res_x_out, res_x_in, res_out, res_in,
    w_sem, s1, r1, s3, r3, ring_s, ring_r, x_s, x_r, core_s, core_r, dw_s, dw_r, da_s, da_r, db_s, db_r, dz_s, dz_r,
    ex_s, ex_r, ch_s, ch_r, xx_s, xx_r, hm_s, hm_r,
):
    e, h = lax.axis_index("expert"), lax.axis_index("hidden")
    z, xl, c = e // 4, (e // 2) % 2, e % 2
    feat = tok_ref.shape[1]
    hid = gg.shape[1]

    def at_z(k):
        return lax.rem(z + (k + NZ) % NZ, NZ)

    def dev(zz, xx, cc, hh):
        return (zz * 4 + xx * 2 + cc, hh)

    def ring(k):
        return dev(at_z(k), xl, c, h)

    x_dev, core_dev = dev(z, 1 - xl, c, h), dev(z, xl, 1 - c, h)

    def remote(src, dst, send, recv, to):
        return pltpu.make_async_remote_copy(
            src_ref=src, dst_ref=dst, send_sem=send, recv_sem=recv, device_id=to, device_id_type=MESH
        )

    sent = []

    def start(*args):
        copy = remote(*args)
        copy.start()
        sent.append(copy)

    def arrived(dst, recv):
        remote(dst, dst, recv, recv, core_dev).wait_recv()

    loads = [
        pltpu.make_async_copy(src.at[0], dst, w_sem.at[i])
        for i, (src, dst) in enumerate(((wg_hbm, wg), (wu_hbm, wu), (wd_hbm, wd)))
    ]
    for load in loads:
        load.start()

    barrier = pltpu.get_barrier_semaphore()

    def greet(to):
        pl.semaphore_signal(barrier, inc=1, device_id=to, device_id_type=MESH)

    for k in range(1, NZ):
        greet(ring(k))
    for k in range(1, NH):
        greet((e, lax.rem(h + k, NH)))
    greet(x_dev)
    greet(core_dev)

    def home_from(k):
        zs = at_z(-k)
        return dev(zs, xl, c, lax.rem(h + zs, NH))

    for k in range(1, NZ):
        greet(home_from(k))

    @pl.when(z != 0)
    def _():
        greet(home_from(0))

    toks[xl, z] = jnp.concatenate([tok_ref[...].astype(F32), cot_ref[...].astype(F32)], 0).astype(BF)
    cols = NZ * BLOCK
    t, lane = iota((TOK, cols), 0), iota((TOK, cols), 1)
    here = jnp.where(lane % TOK == t, 1.0, 0.0)

    def along(values):
        return jnp.dot(values, here, precision=lax.Precision.HIGHEST, preferred_element_type=F32)

    ids_along = along(ids_ref[...].astype(F32)) + 1.0
    own_ids = [ids_along[k : k + 1] for k in range(2)]
    masked = [jnp.where(iota((1, cols), 1) // BLOCK == z, v, 0.0) for v in own_ids]
    lines = [v[:, 128 * k : 128 * k + 128] for v in masked for k in range(3)]
    meta[xl, z] = jnp.concatenate(lines + [jnp.zeros((2, 128), F32)], axis=0)
    hpad = dense_w.shape[2]
    zero = jnp.zeros((hpad - hid, feat), F32)
    for k, ref in enumerate((dg_ref, du_ref, dd_ref)):
        dense_w[k, c] = jnp.concatenate([ref[...].astype(F32), zero], 0).astype(BF)

    pl.semaphore_wait(barrier, (NZ - 1) + (NH - 1) + 2 + (NZ - 1) + (z + NZ - 1) // NZ)

    def zpos(p):
        return at_z(-p) if p <= 4 else at_z(p - 4)

    def token_send(x, p, sems, to):
        send, recv = sems
        zs = zpos(p)
        start(toks.at[x, zs], toks.at[x, zs], send.at[0], recv.at[0], to)
        start(meta.at[x, zs], meta.at[x, zs], send.at[1], recv.at[1], to)

    def token_wait(x, p, recv):
        zs = zpos(p)
        arrived(toks.at[x, zs], recv.at[0])
        arrived(meta.at[x, zs], recv.at[1])

    def token_sems(d, step):
        i = (1 - d) // 2
        return s1.at[i, step - 1], r1.at[i, step - 1]

    def token_hop(d, step):
        p = 0 if step == 1 else (step - 1 if d == 1 else step + 3)
        token_send(xl, p, token_sems(d, step), ring(d))

    def token_arrival(d, step):
        token_wait(xl, step if d == 1 else step + 4, token_sems(d, step)[1])

    def token_x(p):
        token_send(xl, p, (x_s.at[p], x_r.at[p]), x_dev)

    token_x(0)
    token_hop(1, 1)
    token_hop(-1, 1)
    for k in range(3):
        start(dense_w.at[k, c], dense_w.at[k, c], dw_s.at[k], dw_r.at[k], core_dev)
    for step in range(1, 5):
        for d in (1, -1):
            if step == 4 and d == -1:
                continue
            token_arrival(d, step)
            if step < 3 or step == 3 and d == 1:
                token_hop(d, step + 1)
            token_x(step if d == 1 else step + 4)

    y, xh = h // 2, h % 2
    par = z % 2

    def plane(dy, flip):
        return lax.rem(y + dy + 8, 4) * 2 + (1 - xh if flip else xh)

    def column(o):
        return 1 - xl if o else xl

    targets = ((plane(-z, True), 0), (plane(-z, True), 1), (plane(1, False), 1 - par), (plane(-1, False), par), (plane(2, False), par))
    row = iota((8, cols), 0)
    label = jnp.full((8, cols), -1, jnp.int32)
    for i, (q, _) in enumerate(targets + ((h, 0),)):
        label = jnp.where(row == i, q + 1, label)
    label = label.astype(F32)
    a, b = iota((cols, cols), 0), iota((cols, cols), 1)
    before = jnp.where(a // TOK == b // TOK, jnp.where(a < b, 1.0, 0.0), 0.0).astype(BF)
    r, t = iota((PIECE, cols), 0), iota((PIECE, cols), 1)
    slot = (r % CAP).astype(F32)
    group, base = t // TOK, r // CAP * 2

    slices = (
        h, plane(2, False), plane(-1, False), plane(1, False),
        plane(z, True), plane(z - 1, True), plane(z + 1, True), plane(z + 2, True),
    )

    def tensor(p, j):
        if p in (1, 3):
            return 1 - par if j else par
        if p == 2:
            return par if j else 1 - par
        return j

    def chunk(p, k):
        return rows.at[slices[p], c, tensor(p, k // 2), column(k % 2)]

    def core_send(p, k):
        start(chunk(p, k), chunk(p, k), core_s.at[p, k], core_r.at[p, k], core_dev)

    def hop(d, p, k, i):
        j = (1 - d) // 2
        start(chunk(p, k), chunk(p, k), ring_s.at[j, i], ring_r.at[j, i], ring(d))

    for o in range(2):
        x = column(o)
        if o:
            for p in (0, 1, 5, 2, 6, 3, 7, 4):
                token_wait(x, p, x_r.at[p])
        info = meta[x, 0]
        for k in range(1, NZ):
            info = info + meta[x, k]
        ids = [jnp.concatenate([info[i : i + 1] for i in range(3 * k, 3 * k + 3)], axis=1) for k in range(2)]
        match = jnp.where(ids[0] == label, 1.0, jnp.where(ids[1] == label, 1.0, 0.0))
        rank = jnp.dot(match.astype(BF), before, preferred_element_type=F32)
        every = toks[x].reshape(cols, feat)

        def chosen(i, which):
            choose = jnp.where(rank[i : i + 1] == slot, match[i : i + 1], 0.0)
            choose = jnp.where(group == base + which, choose, 0.0).astype(BF)
            return jnp.dot(choose, every, preferred_element_type=F32).astype(BF)

        for i, (q, which) in enumerate(targets):
            pick[i, o] = chosen(i, which)
            start(pick.at[i, o], rows.at[h, c, which, x], s3.at[i, o], r3.at[i, o], (e, q))
        for k in range(2):
            rows[h, c, k, x] = chosen(len(targets), k)
            core_send(0, 2 * k + o)

    def accumulate(p, first=False):
        for k in range(4):
            arrived(rows.at[slices[p], 1 - c, tensor(p, k // 2), column(k % 2)], core_r.at[p, k])
        sl = slices[p]
        col = pl.ds(pl.multiple_of(sl * feat, 128), feat)
        x = rows[sl, :, 0].reshape(4 * PIECE, feat)
        y = rows[sl, :, 1].reshape(4 * PIECE, feat)
        for k, (lhs, w) in enumerate(((x, wg), (x, wu), (y, wd))):
            new = lax.dot_general(lhs, w[:, col], NT, preferred_element_type=F32)
            pre[k] = new if first else pre[k] + new

    def dense_part():
        for k in range(3):
            arrived(dense_w.at[k, 1 - c], dw_r.at[k])
        every = toks[...].reshape(2 * cols, feat)
        for k in range(3):
            w = dense_w[k].reshape(2 * hpad, feat)
            part = lax.dot_general(every, w, NT, preferred_element_type=F32).reshape(2, NZ, BLOCK, 2 * hpad)
            part = part[:, :, 0:TOK] if k < 2 else part[:, :, TOK:BLOCK]
            for hh in range(NH):
                part_out[hh, k] = jnp.concatenate([part[0, hh], part[1, hh]], 0).astype(BF)
        for k in range(1, NH):
            hh = lax.rem(h + k, NH)
            start(part_out.at[hh], part_in.at[k], da_s.at[k], da_r.at[k], (e, hh))

    for o in range(2):
        for k in range(2):
            arrived(chunk(4, 2 * k + o), r3.at[k, o])
            hop(1, 4, 2 * k + o, 2 * k + o)
            hop(-1, 4, 2 * k + o, 2 * k + o)
            core_send(4, 2 * k + o)
        for m, p, d in ((2, 2, -1), (3, 3, 1)):
            arrived(chunk(p, o), r3.at[m, o])
            hop(d, p, o, 6 + o)
            core_send(p, o)
        arrived(chunk(1, o), r3.at[4, o])
        hop(-1 if o else 1, 1, o, 8)
        core_send(1, o)

    dense_part()
    for load in loads:
        load.wait()
    for o in range(2):
        for k in range(2):
            for d in (1, -1):
                p = 5 if d == 1 else 6
                arrived(chunk(p, 2 * k + o), ring_r.at[(1 - d) // 2, 2 * k + o])
                if (k == 0) == (d == 1):
                    hop(d, p, 2 * k + o, 4 + o)
                core_send(p, 2 * k + o)
        if o == 0:
            accumulate(0, True)
    for o in range(2):
        for p, d in ((2, 1), (3, -1)):
            other = 5 - p
            arrived(chunk(other, 2 + o), ring_r.at[(1 - d) // 2, 6 + o])
            core_send(other, 2 + o)
        arrived(chunk(1, 2 + o), ring_r.at[o, 8])
        core_send(1, 2 + o)
    accumulate(4)
    accumulate(5)
    accumulate(6)
    for k in range(2):
        for o in range(2):
            arrived(chunk(7, 2 * k + o), ring_r.at[k, 4 + o])
            core_send(7, 2 * k + o)
        accumulate(3 - k)
    accumulate(1)
    accumulate(7)

    def dense_sum():
        sums = part_out[h].astype(F32)
        for k in range(1, NH):
            arrived(part_in.at[k], da_r.at[k])
            sums = sums + part_in[k].astype(F32)
        dense_gate, dense_up = grads_of(sums[0], sums[1], sums[2])
        dgrad[0, h] = dense_gate
        dgrad[1, h] = dense_up
        for k in range(1, NH):
            start(dgrad.at[:, h], dgrad.at[:, h], db_s.at[k], db_r.at[k], (e, lax.rem(h + k, NH)))

    def dense_result():
        for k in range(1, NH):
            arrived(dgrad.at[:, lax.rem(h + NH - k, NH)], db_r.at[k])
        result = None
        for k in range(2):
            lhs = dgrad[k].reshape(cols, 2 * hpad)
            term = jnp.dot(lhs, dense_w[k].reshape(2 * hpad, feat), preferred_element_type=F32)
            result = term if result is None else result + term
        result = result.reshape(NZ, 2, TOK, feat)
        for x in range(2):
            res[x] = result[:, x]
        res_x_out[...] = res[1 - xl].reshape(NZ * TOK, feat).astype(BF)
        start(res_x_out, res_x_in, xx_s.at[1], xx_r.at[1], x_dev)

    def dense_reduce():
        arrived(res_x_in, xx_r.at[1])
        result = res[xl] + res_x_in[...].astype(F32).reshape(NZ, TOK, feat)
        res[xl] = result
        zero = jnp.zeros((PAD - TOK, feat), F32)
        for k in range(NZ):
            res_out[k] = jnp.concatenate([result[k], zero], 0).astype(BF)
        for k in range(1, NZ):
            start(res_out.at[at_z(k)], res_in.at[k], dz_s.at[k], dz_r.at[k], ring(k))

    new_gate, new_up = grads_of(pre[0], pre[1], pre[2])
    gg[...] = new_gate
    gu[...] = new_up

    def slot_z(i):
        odd = i % 2
        return lax.rem(z + odd * (4 - (i + 1) // 2) + (1 - odd) * (4 + i // 2), NZ)

    half = 2 * PIECE

    def produce(i):
        zd = slot_z(i)
        col = pl.ds(pl.multiple_of(lax.rem(h - zd + NH, NH) * feat, 128), feat)

        def rows_of(cc):
            sel = pl.ds(pl.multiple_of(cc * half, half), half)
            return jnp.dot(gg[sel], wg[:, col], preferred_element_type=F32) + jnp.dot(
                gu[sel], wu[:, col], preferred_element_type=F32
            )

        give[i] = rows_of(1 - c).astype(BF).reshape(2, PIECE, feat)
        start(give.at[i], got.at[i], ex_s.at[i], ex_r.at[i], core_dev)
        keep[i] = rows_of(c).reshape(2, PIECE, feat)

    def mine(i, x):
        return keep[i, x] + got[i, x].astype(F32)

    def chain(d, step, x, i):
        k = (1 - d) // 2
        value = mine(i, x)
        if step == 1 and x == k or step > 1:
            arrived(chain_in.at[k, step - 1, x], ch_r.at[k, step - 1, x])
            value = value + chain_in[k, step - 1, x].astype(F32)
        chain_out[k, step, x] = value.astype(BF)
        start(chain_out.at[k, step, x], chain_in.at[k, step, x], ch_s.at[k, step, x], ch_r.at[k, step, x], ring(d))

    def exchanged(i):
        arrived(got.at[i], ex_r.at[i])

    dense_sum()
    produce(0)
    produce(1)
    exchanged(0)
    chain(1, 0, 0, 0)
    chain(-1, 0, 1, 0)
    produce(2)
    for step in range(1, 4):
        i = 2 * step - 1
        exchanged(i)
        if step == 1:
            chain(1, 1, 1, i)
        produce(i + 2)
        exchanged(i + 1)
        if step == 1:
            chain(-1, 1, 0, i + 1)
            chain(1, 1, 0, i)
            chain(-1, 1, 1, i + 1)
        else:
            for x in (1, 0):
                chain(1, step, x, i)
                chain(-1, step, 1 - x, i + 1)
        if i + 3 < 8:
            produce(i + 3)
        if step == 2:
            dense_result()
    exchanged(7)
    for x in range(2):
        value = mine(7, x)
        for k in range(2):
            arrived(chain_in.at[k, 3, x], ch_r.at[k, 3, x])
            value = value + chain_in[k, 3, x].astype(F32)
        total[x] = value
    x_out[...] = total[1 - xl].astype(BF)
    start(x_out, x_in, xx_s.at[0], xx_r.at[0], x_dev)
    dense_reduce()
    r, t = iota((NZ * 16, PIECE), 0), iota((NZ * 16, PIECE), 1)
    spread = jnp.where(r % 16 < CAP, jnp.where(t == (r // 16) * CAP + r % 16, 1.0, 0.0), 0.0).astype(BF)
    arrived(x_in, xx_r.at[0])
    final = (total[xl] + x_in[...].astype(F32)).astype(BF)
    home_out[...] = jnp.dot(spread, final, preferred_element_type=F32).astype(BF).reshape(NZ, 16, feat)

    back = lax.rem(h - z + NH, NH)
    for k in range(1, NZ):
        zt = at_z(k)
        start(home_out.at[zt], home_in.at[k], hm_s.at[k], hm_r.at[k], dev(zt, xl, c, back))
    home = remote(home_out.at[z], home_in.at[0], hm_s.at[0], hm_r.at[0], dev(z, xl, c, back))
    stay = pltpu.make_async_copy(home_out.at[z], home_in.at[0], hm_r.at[8])

    @pl.when(z != 0)
    def _():
        home.start()

    @pl.when(z == 0)
    def _():
        stay.start()

    n = NZ * 16
    ids0, ids1 = own_ids[0][:, 0:n], own_ids[1][:, 0:n]
    gates = along(gates_ref[...])
    g0, g1 = gates[0:1, 0:n], gates[1:2, 0:n]
    r, t = iota((n, n), 0), iota((n, n), 1)
    label = ((h + (z - r // 16 + NZ) % NZ) % NH + 1).astype(F32)
    hit0, hit1 = jnp.where(ids0 == label, 1.0, 0.0), jnp.where(ids1 == label, 1.0, 0.0)
    before = jnp.where(r // TOK == t // TOK, jnp.where(r < t, 1.0, 0.0), 0.0).astype(BF)
    rank = jnp.dot((hit0 + hit1).astype(BF), before, preferred_element_type=F32)
    weigh = jnp.where(rank == (r % 16).astype(F32), hit0 * g0 + hit1 * g1, 0.0)

    dense = res[xl, z]
    for k in range(1, NZ):
        arrived(res_in.at[k], dz_r.at[k])
        dense = dense + res_in[k, 0:TOK].astype(F32)

    for k in range(1, NZ):
        arrived(home_in.at[k], hm_r.at[k])

    @pl.when(z != 0)
    def _():
        home.wait()

    @pl.when(z == 0)
    def _():
        stay.wait()

    expert = lax.dot_general(
        weigh, home_in[...].reshape(n, feat).astype(F32), (((0,), (0,)), ((), ())),
        precision=lax.Precision.HIGHEST, preferred_element_type=F32,
    )
    out_ref[...] = (cot_ref[...].astype(F32) + dense + expert[0:TOK]).astype(BF)

    for copy in sent:
        copy.wait_send()


def on_device(tokens, cotangent, route_ids, route_gates, expert_gate, expert_up, expert_down, dense_gate, dense_up, dense_down):
    feat = tokens.shape[1]
    hid, width = expert_gate.shape[1], expert_gate.shape[2]
    hpad = (hid + 15) // 16 * 16
    dma, vmem = pltpu.SemaphoreType.DMA, pltpu.VMEM
    scratch = [
        vmem((hid, width), BF), vmem((hid, width), BF), vmem((hid, width), BF),
        vmem((2, NZ, BLOCK, feat), BF),
        vmem((2, NZ, 8, 128), F32),
        vmem((5, 2, PIECE, feat), BF),
        vmem((NH, 2, 2, 2, PIECE, feat), BF),
        vmem((3, 4 * PIECE, hid), F32),
        vmem((4 * PIECE, hid), BF), vmem((4 * PIECE, hid), BF),
        vmem((NZ, 2, PIECE, feat), F32),
        vmem((NZ, 2, PIECE, feat), BF), vmem((NZ, 2, PIECE, feat), BF),
        vmem((2, 4, 2, PIECE, feat), BF), vmem((2, 4, 2, PIECE, feat), BF),
        vmem((2, PIECE, feat), F32),
        vmem((PIECE, feat), BF), vmem((PIECE, feat), BF),
        vmem((NZ, 16, feat), BF), vmem((NZ, 16, feat), BF),
        vmem((3, 2, hpad, feat), BF),
        vmem((NH, 3, BLOCK, 2 * hpad), BF), vmem((NH, 3, BLOCK, 2 * hpad), BF),
        vmem((2, NH, BLOCK, 2 * hpad), BF),
        vmem((2, NZ, TOK, feat), F32),
        vmem((NZ * TOK, feat), BF), vmem((NZ * TOK, feat), BF),
        vmem((NZ, PAD, feat), BF), vmem((NZ, PAD, feat), BF),
        dma((3,)), dma((2, 4, 2)), dma((2, 4, 2)), dma((5, 2)), dma((5, 2)),
        dma((2, 9)), dma((2, 9)), dma((8, 2)), dma((8, 2)), dma((8, 4)), dma((8, 4)),
        dma((3,)), dma((3,)), dma((8,)), dma((8,)), dma((8,)), dma((8,)), dma((8,)), dma((8,)),
        dma((8,)), dma((8,)), dma((2, 4, 2)), dma((2, 4, 2)), dma((2,)), dma((2,)), dma((9,)), dma((9,)),
    ]
    whole, far = pl.BlockSpec(memory_space=pltpu.VMEM), pl.BlockSpec(memory_space=pl.ANY)
    return pl.pallas_call(
        kernel,
        out_shape=jax.ShapeDtypeStruct(tokens.shape, BF),
        in_specs=[whole] * 4 + [far] * 3 + [whole] * 3,
        out_specs=whole,
        scratch_shapes=scratch,
        compiler_params=pltpu.CompilerParams(collective_id=0, has_side_effects=True, vmem_limit_bytes=56 << 20),
        name="layer",
    )(tokens, cotangent, route_ids.T, route_gates.T, expert_gate, expert_up, expert_down, dense_gate, dense_up, dense_down)


def solution(mesh):
    in_specs = (
        P("expert", "hidden"),
        P("expert", "hidden"),
        P("expert", None),
        P("expert", None),
        P("hidden", "expert", None),
        P("hidden", "expert", None),
        P("hidden", "expert", None),
        P("expert", "hidden"),
        P("expert", "hidden"),
        P("expert", "hidden"),
    )
    return jax.shard_map(on_device, mesh=mesh, in_specs=in_specs, out_specs=P("expert", "hidden"), check_vma=False)
```

```python
import functools

import jax
import jax.numpy as jnp
from jax import lax
from jax.experimental import pallas as pl
from jax.experimental.pallas import tpu as pltpu
from jax.sharding import PartitionSpec as P

MESH = pl.DeviceIdType.MESH
BF, F32 = jnp.bfloat16, jnp.float32
NZ, NH = 8, 8
TOK, PAD = 24, 32
BLOCK = 2 * TOK
CAP = 10
PIECE = NZ * CAP
NT = (((1,), (1,)), ((), ()))


def grads_of(pre_gate, pre_up, upstream):
    sigma = 1.0 / (1.0 + jnp.exp(-pre_gate))
    grad_gate = upstream * pre_up * sigma * (1.0 + pre_gate * (1.0 - sigma))
    grad_up = upstream * pre_gate * sigma
    return grad_gate.astype(BF), grad_up.astype(BF)


def iota(shape, dim):
    return lax.broadcasted_iota(jnp.int32, shape, dim)


def kernel(
    tok_ref, cot_ref, ids_ref, gates_ref, wg_hbm, wu_hbm, wd_hbm, dg_ref, du_ref, dd_ref, out_ref,
    wg, wu, wd, toks, meta, pick, rows, pre, gg, gu, keep, give, got, chain_out, chain_in, side_out, side_in, rest_out, rest_in, total,
    x_out, x_in, home_out, home_in, dense_w, part_out, part_in, dgrad, res, res_x_out, res_x_in, res_out, res_in,
    w_sem, s1, r1, s3, r3, ring_s, ring_r, x_s, x_r, core_s, core_r, dw_s, dw_r, da_s, da_r, db_s, db_r, dz_s, dz_r,
    ex_s, ex_r, ch_s, ch_r, sd_s, sd_r, rs_s, rs_r, xx_s, xx_r, hm_s, hm_r,
):
    e, h = lax.axis_index("expert"), lax.axis_index("hidden")
    z, xl, c = e // 4, (e // 2) % 2, e % 2
    feat = tok_ref.shape[1]
    hid = gg.shape[1]

    def at_z(k):
        return lax.rem(z + (k + NZ) % NZ, NZ)

    def dev(zz, xx, cc, hh):
        return (zz * 4 + xx * 2 + cc, hh)

    def ring(k):
        return dev(at_z(k), xl, c, h)

    x_dev, core_dev = dev(z, 1 - xl, c, h), dev(z, xl, 1 - c, h)

    def remote(src, dst, send, recv, to):
        return pltpu.make_async_remote_copy(
            src_ref=src, dst_ref=dst, send_sem=send, recv_sem=recv, device_id=to, device_id_type=MESH
        )

    sent = []

    def start(*args):
        copy = remote(*args)
        copy.start()
        sent.append(copy)

    def arrived(dst, recv):
        remote(dst, dst, recv, recv, core_dev).wait_recv()

    loads = [
        pltpu.make_async_copy(src.at[0], dst, w_sem.at[i])
        for i, (src, dst) in enumerate(((wg_hbm, wg), (wu_hbm, wu), (wd_hbm, wd)))
    ]
    for load in loads:
        load.start()

    barrier = pltpu.get_barrier_semaphore()

    def greet(to):
        pl.semaphore_signal(barrier, inc=1, device_id=to, device_id_type=MESH)

    for k in range(1, NZ):
        greet(ring(k))
    for k in range(1, NH):
        greet((e, lax.rem(h + k, NH)))
    greet(x_dev)
    greet(core_dev)

    def home_from(k):
        zs = at_z(-k)
        return dev(zs, xl, c, lax.rem(h + zs, NH))

    for k in range(1, NZ):
        greet(home_from(k))

    @pl.when(z != 0)
    def _():
        greet(home_from(0))

    toks[xl, z] = jnp.concatenate([tok_ref[...].astype(F32), cot_ref[...].astype(F32)], 0).astype(BF)
    cols = NZ * BLOCK
    t, lane = iota((TOK, cols), 0), iota((TOK, cols), 1)
    here = jnp.where(lane % TOK == t, 1.0, 0.0)

    def along(values):
        return jnp.dot(values, here, precision=lax.Precision.HIGHEST, preferred_element_type=F32)

    ids_along = along(ids_ref[...].astype(F32)) + 1.0
    own_ids = [ids_along[k : k + 1] for k in range(2)]
    masked = [jnp.where(iota((1, cols), 1) // BLOCK == z, v, 0.0) for v in own_ids]
    lines = [v[:, 128 * k : 128 * k + 128] for v in masked for k in range(3)]
    meta[xl, z] = jnp.concatenate(lines + [jnp.zeros((2, 128), F32)], axis=0)
    hpad = dense_w.shape[2]
    zero = jnp.zeros((hpad - hid, feat), F32)
    for k, ref in enumerate((dg_ref, du_ref, dd_ref)):
        dense_w[k, c] = jnp.concatenate([ref[...].astype(F32), zero], 0).astype(BF)

    pl.semaphore_wait(barrier, (NZ - 1) + (NH - 1) + 2 + (NZ - 1) + (z + NZ - 1) // NZ)

    def zpos(p):
        return at_z(-p) if p <= 4 else at_z(p - 4)

    def token_parts(x, p):
        zs = zpos(p)
        return [meta.at[x, zs]] + [toks.at[x, zs, pl.ds(16 * k, 16)] for k in range(BLOCK // 16)]

    def token_send(x, p, sems, to):
        for k, ref in enumerate(token_parts(x, p)):
            start(ref, ref, sems[0].at[k], sems[1].at[k], to)

    def token_wait(x, p, recv):
        for k, ref in enumerate(token_parts(x, p)):
            arrived(ref, recv.at[k])

    def token_sems(d, step):
        i = (1 - d) // 2
        return s1.at[i, step - 1], r1.at[i, step - 1]

    def token_pass(d, step):
        p = step + 4 if d == -1 and step else step
        for k, ref in enumerate(token_parts(xl, p)):
            if step:
                arrived(ref, token_sems(d, step)[1].at[k])
            if step < (4 if d == 1 else 3):
                send, recv = token_sems(d, step + 1)
                start(ref, ref, send.at[k], recv.at[k], ring(d))

    def token_x(p):
        token_send(xl, p, (x_s.at[p], x_r.at[p]), x_dev)

    token_pass(1, 0)
    token_pass(-1, 0)
    token_x(0)
    for k in range(3):
        start(dense_w.at[k, c], dense_w.at[k, c], dw_s.at[k], dw_r.at[k], core_dev)
    for step in range(1, 5):
        for d in (1, -1):
            if step == 4 and d == -1:
                continue
            token_pass(d, step)
            token_x(step if d == 1 else step + 4)

    y, xh = h // 2, h % 2
    par = z % 2

    def plane(dy, flip):
        return lax.rem(y + dy + 8, 4) * 2 + (1 - xh if flip else xh)

    def column(o):
        return 1 - xl if o else xl

    targets = ((plane(-z, True), 0), (plane(-z, True), 1), (plane(1, False), 1 - par), (plane(-1, False), par), (plane(2, False), par))
    row = iota((8, cols), 0)
    label = jnp.full((8, cols), -1, jnp.int32)
    for i, (q, _) in enumerate(targets + ((h, 0),)):
        label = jnp.where(row == i, q + 1, label)
    label = label.astype(F32)
    a, b = iota((cols, cols), 0), iota((cols, cols), 1)
    before = jnp.where(a // TOK == b // TOK, jnp.where(a < b, 1.0, 0.0), 0.0).astype(BF)
    r, t = iota((PIECE, cols), 0), iota((PIECE, cols), 1)
    slot = (r % CAP).astype(F32)
    group, base = t // TOK, r // CAP * 2

    slices = (
        h, plane(2, False), plane(-1, False), plane(1, False),
        plane(z, True), plane(z - 1, True), plane(z + 1, True), plane(z + 2, True),
    )

    def tensor(p, j):
        if p in (1, 3):
            return 1 - par if j else par
        if p == 2:
            return par if j else 1 - par
        return j

    def chunk(p, k):
        return rows.at[slices[p], c, tensor(p, k // 2), column(k % 2)]

    def core_send(p, k):
        start(chunk(p, k), chunk(p, k), core_s.at[p, k], core_r.at[p, k], core_dev)

    def hop(d, p, k, i):
        j = (1 - d) // 2
        start(chunk(p, k), chunk(p, k), ring_s.at[j, i], ring_r.at[j, i], ring(d))

    for o in range(2):
        x = column(o)
        if o:
            for p in (0, 1, 5, 2, 6, 3, 7, 4):
                token_wait(x, p, x_r.at[p])
        info = meta[x, 0]
        for k in range(1, NZ):
            info = info + meta[x, k]
        ids = [jnp.concatenate([info[i : i + 1] for i in range(3 * k, 3 * k + 3)], axis=1) for k in range(2)]
        match = jnp.where(ids[0] == label, 1.0, jnp.where(ids[1] == label, 1.0, 0.0))
        rank = jnp.dot(match.astype(BF), before, preferred_element_type=F32)
        every = toks[x].reshape(cols, feat)

        def chosen(i, which):
            choose = jnp.where(rank[i : i + 1] == slot, match[i : i + 1], 0.0)
            choose = jnp.where(group == base + which, choose, 0.0).astype(BF)
            return jnp.dot(choose, every, preferred_element_type=F32).astype(BF)

        for i, (q, which) in enumerate(targets):
            pick[i, o] = chosen(i, which)
            start(pick.at[i, o], rows.at[h, c, which, x], s3.at[i, o], r3.at[i, o], (e, q))
        for k in range(2):
            rows[h, c, k, x] = chosen(len(targets), k)
            core_send(0, 2 * k + o)

    def accumulate(p, first=False):
        for k in range(4):
            arrived(rows.at[slices[p], 1 - c, tensor(p, k // 2), column(k % 2)], core_r.at[p, k])
        sl = slices[p]
        col = pl.ds(pl.multiple_of(sl * feat, 128), feat)
        x = rows[sl, :, 0].reshape(4 * PIECE, feat)
        y = rows[sl, :, 1].reshape(4 * PIECE, feat)
        for k, (lhs, w) in enumerate(((x, wg), (x, wu), (y, wd))):
            new = lax.dot_general(lhs, w[:, col], NT, preferred_element_type=F32)
            pre[k] = new if first else pre[k] + new

    def dense_part():
        for k in range(3):
            arrived(dense_w.at[k, 1 - c], dw_r.at[k])
        every = toks[...].reshape(2 * cols, feat)
        for k in range(3):
            w = dense_w[k].reshape(2 * hpad, feat)
            part = lax.dot_general(every, w, NT, preferred_element_type=F32).reshape(2, NZ, BLOCK, 2 * hpad)
            part = part[:, :, 0:TOK] if k < 2 else part[:, :, TOK:BLOCK]
            for hh in range(NH):
                part_out[hh, k] = jnp.concatenate([part[0, hh], part[1, hh]], 0).astype(BF)
        for k in range(1, NH):
            hh = lax.rem(h + k, NH)
            start(part_out.at[hh], part_in.at[k], da_s.at[k], da_r.at[k], (e, hh))

    for o in range(2):
        for k in range(2):
            arrived(chunk(4, 2 * k + o), r3.at[k, o])
            hop(1, 4, 2 * k + o, 2 * k + o)
            hop(-1, 4, 2 * k + o, 2 * k + o)
            core_send(4, 2 * k + o)
        for m, p, d in ((2, 2, -1), (3, 3, 1)):
            arrived(chunk(p, o), r3.at[m, o])
            hop(d, p, o, 6 + o)
            core_send(p, o)
        arrived(chunk(1, o), r3.at[4, o])
        hop(-1 if o else 1, 1, o, 8)
        core_send(1, o)

    dense_part()
    for load in loads:
        load.wait()
    for o in range(2):
        for k in range(2):
            for d in (1, -1):
                p = 5 if d == 1 else 6
                arrived(chunk(p, 2 * k + o), ring_r.at[(1 - d) // 2, 2 * k + o])
                if (k == 0) == (d == 1):
                    hop(d, p, 2 * k + o, 4 + o)
                core_send(p, 2 * k + o)
        if o == 0:
            accumulate(0, True)
    for o in range(2):
        for p, d in ((2, 1), (3, -1)):
            other = 5 - p
            arrived(chunk(other, 2 + o), ring_r.at[(1 - d) // 2, 6 + o])
            core_send(other, 2 + o)
        arrived(chunk(1, 2 + o), ring_r.at[o, 8])
        core_send(1, 2 + o)
    accumulate(4)
    accumulate(5)
    accumulate(6)
    for k in range(2):
        for o in range(2):
            arrived(chunk(7, 2 * k + o), ring_r.at[k, 4 + o])
            core_send(7, 2 * k + o)
        accumulate(3 - k)
    accumulate(1)
    accumulate(7)

    def dense_sum():
        sums = part_out[h].astype(F32)
        for k in range(1, NH):
            arrived(part_in.at[k], da_r.at[k])
            sums = sums + part_in[k].astype(F32)
        dense_gate, dense_up = grads_of(sums[0], sums[1], sums[2])
        dgrad[0, h] = dense_gate
        dgrad[1, h] = dense_up
        start(dgrad.at[:, h], dgrad.at[:, h], db_s.at[0], db_r.at[0], (e, plane(0, True)))
        for k in range(1, 4):
            start(dgrad.at[:, h], dgrad.at[:, h], db_s.at[k], db_r.at[k], (e, plane(k, False)))

    def dense_pass():
        ref = dgrad.at[:, plane(0, True)]
        arrived(ref, db_r.at[0])
        for k in range(1, 4):
            start(ref, ref, db_s.at[3 + k], db_r.at[3 + k], (e, plane(k, False)))

    def dense_result():
        for k in range(1, 4):
            arrived(dgrad.at[:, plane(-k, False)], db_r.at[k])
            arrived(dgrad.at[:, plane(-k, True)], db_r.at[3 + k])
        result = None
        for k in range(2):
            lhs = dgrad[k].reshape(cols, 2 * hpad)
            term = jnp.dot(lhs, dense_w[k].reshape(2 * hpad, feat), preferred_element_type=F32)
            result = term if result is None else result + term
        result = result.reshape(NZ, 2, TOK, feat)
        for x in range(2):
            res[x] = result[:, x]
        res_x_out[...] = res[1 - xl].reshape(NZ * TOK, feat).astype(BF)
        start(res_x_out, res_x_in, xx_s.at[1], xx_r.at[1], x_dev)

    def dense_reduce():
        arrived(res_x_in, xx_r.at[1])
        result = res[xl] + res_x_in[...].astype(F32).reshape(NZ, TOK, feat)
        res[xl] = result
        zero = jnp.zeros((PAD - TOK, feat), F32)
        for k in range(NZ):
            res_out[k] = jnp.concatenate([result[k], zero], 0).astype(BF)
        for k in range(1, NZ):
            start(res_out.at[at_z(k)], res_in.at[k], dz_s.at[k], dz_r.at[k], ring(k))

    new_gate, new_up = grads_of(pre[0], pre[1], pre[2])
    gg[...] = new_gate
    gu[...] = new_up

    def slot_z(i):
        odd = i % 2
        return lax.rem(z + odd * (4 - (i + 1) // 2) + (1 - odd) * (4 + i // 2), NZ)

    half = 2 * PIECE

    def produce(i):
        zd = slot_z(i)
        col = pl.ds(pl.multiple_of(lax.rem(h - zd + NH, NH) * feat, 128), feat)

        def rows_of(cc):
            sel = pl.ds(pl.multiple_of(cc * half, half), half)
            return jnp.dot(gg[sel], wg[:, col], preferred_element_type=F32) + jnp.dot(
                gu[sel], wu[:, col], preferred_element_type=F32
            )

        give[i] = rows_of(1 - c).astype(BF).reshape(2, PIECE, feat)
        start(give.at[i], got.at[i], ex_s.at[i], ex_r.at[i], core_dev)
        keep[i] = rows_of(c).reshape(2, PIECE, feat)

    cut = chain_out.shape[4]

    def settle(i):
        arrived(got.at[i], ex_r.at[i])
        keep[i] = keep[i] + got[i].astype(F32)
        side_out[i] = keep[i, 1 - xl, :, cut:feat].astype(BF)
        start(side_out.at[i], side_in.at[i], sd_s.at[i], sd_r.at[i], x_dev)

    def chain(d, step, x, i):
        k = (1 - d) // 2
        value = keep[i, x, :, 0:cut]
        if step == 1 and x == k or step > 1:
            arrived(chain_in.at[k, step - 1, x], ch_r.at[k, step - 1, x])
            value = value + chain_in[k, step - 1, x].astype(F32)
        chain_out[k, step, x] = value.astype(BF)
        start(chain_out.at[k, step, x], chain_in.at[k, step, x], ch_s.at[k, step, x], ch_r.at[k, step, x], ring(d))

    def side(i):
        arrived(side_in.at[i], sd_r.at[i])
        return keep[i, xl, :, cut:feat] + side_in[i].astype(F32)

    def side_chain(d, step, i):
        k = (1 - d) // 2
        value = side(i)
        if step > k:
            arrived(rest_in.at[k, step - 1], rs_r.at[k, step - 1])
            value = value + rest_in[k, step - 1].astype(F32)
        rest_out[k, step] = value.astype(BF)
        start(rest_out.at[k, step], rest_in.at[k, step], rs_s.at[k, step], rs_r.at[k, step], ring(d))

    dense_sum()
    produce(0)
    produce(1)
    settle(0)
    chain(1, 0, 0, 0)
    chain(-1, 0, 1, 0)
    produce(2)
    dense_pass()
    for step in range(1, 4):
        i = 2 * step - 1
        settle(i)
        if step == 1:
            chain(1, 1, 1, i)
        produce(i + 2)
        settle(i + 1)
        if step == 1:
            chain(-1, 1, 0, i + 1)
            chain(1, 1, 0, i)
            chain(-1, 1, 1, i + 1)
        else:
            for x in (1, 0):
                chain(1, step, x, i)
                chain(-1, step, 1 - x, i + 1)
        if i + 3 < 8:
            produce(i + 3)
        if step > 1:
            side_chain(-1, step - 1, i - 1)
        side_chain(1, step - 1, max(i - 2, 0))
        if step == 2:
            dense_result()
        if step == 3:
            dense_reduce()
    settle(7)
    for x in range(2):
        value = keep[7, x, :, 0:cut]
        for k in range(2):
            arrived(chain_in.at[k, 3, x], ch_r.at[k, 3, x])
            value = value + chain_in[k, 3, x].astype(F32)
        total[x] = value
    x_out[...] = total[1 - xl].astype(BF)
    start(x_out, x_in, xx_s.at[0], xx_r.at[0], x_dev)
    side_chain(-1, 3, 6)
    side_chain(1, 3, 5)
    rest = side(7)
    for k in range(2):
        arrived(rest_in.at[k, 3], rs_r.at[k, 3])
        rest = rest + rest_in[k, 3].astype(F32)
    r, t = iota((NZ * 16, PIECE), 0), iota((NZ * 16, PIECE), 1)
    spread = jnp.where(r % 16 < CAP, jnp.where(t == (r // 16) * CAP + r % 16, 1.0, 0.0), 0.0).astype(BF)
    arrived(x_in, xx_r.at[0])
    first = total[xl] + x_in[...].astype(F32)
    for lo, hi, value in ((0, cut, first), (cut, feat, rest)):
        home_out[:, :, lo:hi] = jnp.dot(spread, value.astype(BF), preferred_element_type=F32).astype(BF).reshape(NZ, 16, hi - lo)

    back = lax.rem(h - z + NH, NH)
    for k in range(1, NZ):
        zt = at_z(k)
        start(home_out.at[zt], home_in.at[k], hm_s.at[k], hm_r.at[k], dev(zt, xl, c, back))
    home = remote(home_out.at[z], home_in.at[0], hm_s.at[0], hm_r.at[0], dev(z, xl, c, back))
    stay = pltpu.make_async_copy(home_out.at[z], home_in.at[0], hm_r.at[8])

    @pl.when(z != 0)
    def _():
        home.start()

    @pl.when(z == 0)
    def _():
        stay.start()

    n = NZ * 16
    ids0, ids1 = own_ids[0][:, 0:n], own_ids[1][:, 0:n]
    gates = along(gates_ref[...])
    g0, g1 = gates[0:1, 0:n], gates[1:2, 0:n]
    r, t = iota((n, n), 0), iota((n, n), 1)
    label = ((h + (z - r // 16 + NZ) % NZ) % NH + 1).astype(F32)
    hit0, hit1 = jnp.where(ids0 == label, 1.0, 0.0), jnp.where(ids1 == label, 1.0, 0.0)
    before = jnp.where(r // TOK == t // TOK, jnp.where(r < t, 1.0, 0.0), 0.0).astype(BF)
    rank = jnp.dot((hit0 + hit1).astype(BF), before, preferred_element_type=F32)
    weigh = jnp.where(rank == (r % 16).astype(F32), hit0 * g0 + hit1 * g1, 0.0)

    dense = res[xl, z]
    for k in range(1, NZ):
        arrived(res_in.at[k], dz_r.at[k])
        dense = dense + res_in[k, 0:TOK].astype(F32)

    for k in range(1, NZ):
        arrived(home_in.at[k], hm_r.at[k])

    @pl.when(z != 0)
    def _():
        home.wait()

    @pl.when(z == 0)
    def _():
        stay.wait()

    expert = lax.dot_general(
        weigh, home_in[...].reshape(n, feat).astype(F32), (((0,), (0,)), ((), ())),
        precision=lax.Precision.HIGHEST, preferred_element_type=F32,
    )
    out_ref[...] = (cot_ref[...].astype(F32) + dense + expert[0:TOK]).astype(BF)

    for copy in sent:
        copy.wait_send()


def on_device(tokens, cotangent, route_ids, route_gates, expert_gate, expert_up, expert_down, dense_gate, dense_up, dense_down):
    feat = tokens.shape[1]
    hid, width = expert_gate.shape[1], expert_gate.shape[2]
    hpad = (hid + 15) // 16 * 16
    cut = feat // 128 * 4 // 7 * 128
    dma, vmem = pltpu.SemaphoreType.DMA, pltpu.VMEM
    scratch = [
        vmem((hid, width), BF), vmem((hid, width), BF), vmem((hid, width), BF),
        vmem((2, NZ, BLOCK, feat), BF),
        vmem((2, NZ, 8, 128), F32),
        vmem((5, 2, PIECE, feat), BF),
        vmem((NH, 2, 2, 2, PIECE, feat), BF),
        vmem((3, 4 * PIECE, hid), F32),
        vmem((4 * PIECE, hid), BF), vmem((4 * PIECE, hid), BF),
        vmem((NZ, 2, PIECE, feat), F32),
        vmem((NZ, 2, PIECE, feat), BF), vmem((NZ, 2, PIECE, feat), BF),
        vmem((2, 4, 2, PIECE, cut), BF), vmem((2, 4, 2, PIECE, cut), BF),
        vmem((NZ, PIECE, feat - cut), BF), vmem((NZ, PIECE, feat - cut), BF),
        vmem((2, 4, PIECE, feat - cut), BF), vmem((2, 4, PIECE, feat - cut), BF),
        vmem((2, PIECE, cut), F32),
        vmem((PIECE, cut), BF), vmem((PIECE, cut), BF),
        vmem((NZ, 16, feat), BF), vmem((NZ, 16, feat), BF),
        vmem((3, 2, hpad, feat), BF),
        vmem((NH, 3, BLOCK, 2 * hpad), BF), vmem((NH, 3, BLOCK, 2 * hpad), BF),
        vmem((2, NH, BLOCK, 2 * hpad), BF),
        vmem((2, NZ, TOK, feat), F32),
        vmem((NZ * TOK, feat), BF), vmem((NZ * TOK, feat), BF),
        vmem((NZ, PAD, feat), BF), vmem((NZ, PAD, feat), BF),
        dma((3,)), dma((2, 4, 4)), dma((2, 4, 4)), dma((5, 2)), dma((5, 2)),
        dma((2, 9)), dma((2, 9)), dma((8, 4)), dma((8, 4)), dma((8, 4)), dma((8, 4)),
        dma((3,)), dma((3,)), dma((8,)), dma((8,)), dma((8,)), dma((8,)), dma((8,)), dma((8,)),
        dma((8,)), dma((8,)), dma((2, 4, 2)), dma((2, 4, 2)), dma((8,)), dma((8,)), dma((2, 4)), dma((2, 4)),
        dma((2,)), dma((2,)), dma((9,)), dma((9,)),
    ]
    whole, far = pl.BlockSpec(memory_space=pltpu.VMEM), pl.BlockSpec(memory_space=pl.ANY)
    return pl.pallas_call(
        kernel,
        out_shape=jax.ShapeDtypeStruct(tokens.shape, BF),
        in_specs=[whole] * 4 + [far] * 3 + [whole] * 3,
        out_specs=whole,
        scratch_shapes=scratch,
        compiler_params=pltpu.CompilerParams(collective_id=0, has_side_effects=True, vmem_limit_bytes=56 << 20),
        name="layer",
    )(tokens, cotangent, route_ids.T, route_gates.T, expert_gate, expert_up, expert_down, dense_gate, dense_up, dense_down)


def solution(mesh):
    in_specs = (
        P("expert", "hidden"),
        P("expert", "hidden"),
        P("expert", None),
        P("expert", None),
        P("hidden", "expert", None),
        P("hidden", "expert", None),
        P("hidden", "expert", None),
        P("expert", "hidden"),
        P("expert", "hidden"),
        P("expert", "hidden"),
    )
    return jax.shard_map(on_device, mesh=mesh, in_specs=in_specs, out_specs=P("expert", "hidden"), check_vma=False)
```

```python
import functools

import jax
import jax.numpy as jnp
from jax import lax
from jax.experimental import pallas as pl
from jax.experimental.pallas import tpu as pltpu
from jax.sharding import PartitionSpec as P

MESH = pl.DeviceIdType.MESH
BF, F32 = jnp.bfloat16, jnp.float32
NZ, NH = 8, 8
TOK, PAD = 24, 32
BLOCK = 2 * TOK
CAP = 10
PIECE = NZ * CAP
NT = (((1,), (1,)), ((), ()))


def grads_of(pre_gate, pre_up, upstream):
    sigma = 1.0 / (1.0 + jnp.exp(-pre_gate))
    grad_gate = upstream * pre_up * sigma * (1.0 + pre_gate * (1.0 - sigma))
    grad_up = upstream * pre_gate * sigma
    return grad_gate.astype(BF), grad_up.astype(BF)


def iota(shape, dim):
    return lax.broadcasted_iota(jnp.int32, shape, dim)


def kernel(
    tok_ref, cot_ref, ids_ref, gates_ref, wg_hbm, wu_hbm, wd_hbm, dg_ref, du_ref, dd_ref, out_ref,
    wg, wu, wd, toks, meta, pick, rows, pre, gg, gu, keep, give, got, chain_out, chain_in, side_out, side_in, rest_out, rest_in, total,
    x_out, x_in, home_out, home_in, dense_w, part_out, part_in, dgrad, res, res_x_out, res_x_in, res_out, res_in,
    w_sem, s1, r1, s3, r3, ring_s, ring_r, x_s, x_r, core_s, core_r, dw_s, dw_r, da_s, da_r, db_s, db_r, dz_s, dz_r,
    ex_s, ex_r, ch_s, ch_r, sd_s, sd_r, rs_s, rs_r, xx_s, xx_r, hm_s, hm_r,
):
    e, h = lax.axis_index("expert"), lax.axis_index("hidden")
    z, xl, c = e // 4, (e // 2) % 2, e % 2
    feat = tok_ref.shape[1]
    hid = gg.shape[1]

    def at_z(k):
        return lax.rem(z + (k + NZ) % NZ, NZ)

    def dev(zz, xx, cc, hh):
        return (zz * 4 + xx * 2 + cc, hh)

    def ring(k):
        return dev(at_z(k), xl, c, h)

    x_dev, core_dev = dev(z, 1 - xl, c, h), dev(z, xl, 1 - c, h)

    def remote(src, dst, send, recv, to):
        return pltpu.make_async_remote_copy(
            src_ref=src, dst_ref=dst, send_sem=send, recv_sem=recv, device_id=to, device_id_type=MESH
        )

    sent = []

    def start(*args):
        copy = remote(*args)
        copy.start()
        sent.append(copy)

    def arrived(dst, recv):
        remote(dst, dst, recv, recv, core_dev).wait_recv()

    loads = [
        pltpu.make_async_copy(src.at[0], dst, w_sem.at[i])
        for i, (src, dst) in enumerate(((wg_hbm, wg), (wu_hbm, wu), (wd_hbm, wd)))
    ]
    for load in loads:
        load.start()

    barrier = pltpu.get_barrier_semaphore()

    def greet(to):
        pl.semaphore_signal(barrier, inc=1, device_id=to, device_id_type=MESH)

    for k in range(1, NZ):
        greet(ring(k))
    for k in range(1, NH):
        greet((e, lax.rem(h + k, NH)))
    greet(x_dev)
    greet(core_dev)

    def home_from(k):
        zs = at_z(-k)
        return dev(zs, xl, c, lax.rem(h + zs, NH))

    for k in range(1, NZ):
        greet(home_from(k))

    @pl.when(z != 0)
    def _():
        greet(home_from(0))

    toks[xl, z] = jnp.concatenate([tok_ref[...].astype(F32), cot_ref[...].astype(F32)], 0).astype(BF)
    cols = NZ * BLOCK
    t, lane = iota((TOK, cols), 0), iota((TOK, cols), 1)
    here = jnp.where(lane % TOK == t, 1.0, 0.0)

    def along(values):
        return jnp.dot(values, here, precision=lax.Precision.HIGHEST, preferred_element_type=F32)

    ids_along = along(ids_ref[...].astype(F32)) + 1.0
    own_ids = [ids_along[k : k + 1] for k in range(2)]
    masked = [jnp.where(iota((1, cols), 1) // BLOCK == z, v, 0.0) for v in own_ids]
    lines = [v[:, 128 * k : 128 * k + 128] for v in masked for k in range(3)]
    meta[xl, z] = jnp.concatenate(lines + [jnp.zeros((2, 128), F32)], axis=0)
    hpad = dense_w.shape[2]
    zero = jnp.zeros((hpad - hid, feat), F32)
    for k, ref in enumerate((dg_ref, du_ref, dd_ref)):
        dense_w[k, c] = jnp.concatenate([ref[...].astype(F32), zero], 0).astype(BF)

    pl.semaphore_wait(barrier, (NZ - 1) + (NH - 1) + 2 + (NZ - 1) + (z + NZ - 1) // NZ)

    def zpos(p):
        return at_z(-p) if p <= 4 else at_z(p - 4)

    def token_parts(x, p):
        zs = zpos(p)
        return [meta.at[x, zs]] + [toks.at[x, zs, pl.ds(16 * k, 16)] for k in range(BLOCK // 16)]

    def token_send(x, p, sems, to):
        for k, ref in enumerate(token_parts(x, p)):
            start(ref, ref, sems[0].at[k], sems[1].at[k], to)

    def token_wait(x, p, recv):
        for k, ref in enumerate(token_parts(x, p)):
            arrived(ref, recv.at[k])

    def token_sems(d, step):
        i = (1 - d) // 2
        return s1.at[i, step - 1], r1.at[i, step - 1]

    def token_pass(d, step):
        p = step + 4 if d == -1 and step else step
        for k, ref in enumerate(token_parts(xl, p)):
            if step:
                arrived(ref, token_sems(d, step)[1].at[k])
            if step < (4 if d == 1 else 3):
                send, recv = token_sems(d, step + 1)
                start(ref, ref, send.at[k], recv.at[k], ring(d))

    def token_x(p):
        token_send(xl, p, (x_s.at[p], x_r.at[p]), x_dev)

    token_pass(1, 0)
    token_pass(-1, 0)
    token_x(0)
    for k in range(3):
        start(dense_w.at[k, c], dense_w.at[k, c], dw_s.at[k], dw_r.at[k], core_dev)
    for step in range(1, 5):
        for d in (1, -1):
            if step == 4 and d == -1:
                continue
            token_pass(d, step)
            token_x(step if d == 1 else step + 4)

    y, xh = h // 2, h % 2
    par = z % 2

    def plane(dy, flip):
        return lax.rem(y + dy + 8, 4) * 2 + (1 - xh if flip else xh)

    def column(o):
        return 1 - xl if o else xl

    targets = ((plane(-z, True), 0), (plane(-z, True), 1), (plane(1, False), 1 - par), (plane(-1, False), par), (plane(2, False), par))
    row = iota((8, cols), 0)
    label = jnp.full((8, cols), -1, jnp.int32)
    for i, (q, _) in enumerate(targets + ((h, 0),)):
        label = jnp.where(row == i, q + 1, label)
    label = label.astype(F32)
    a, b = iota((cols, cols), 0), iota((cols, cols), 1)
    before = jnp.where(a // TOK == b // TOK, jnp.where(a < b, 1.0, 0.0), 0.0).astype(BF)
    r, t = iota((PIECE, cols), 0), iota((PIECE, cols), 1)
    slot = (r % CAP).astype(F32)
    group, base = t // TOK, r // CAP * 2

    slices = (
        h, plane(2, False), plane(-1, False), plane(1, False),
        plane(z, True), plane(z - 1, True), plane(z + 1, True), plane(z + 2, True),
    )

    def tensor(p, j):
        if p in (1, 3):
            return 1 - par if j else par
        if p == 2:
            return par if j else 1 - par
        return j

    def chunk(p, k):
        return rows.at[slices[p], c, tensor(p, k // 2), column(k % 2)]

    def core_send(p, k):
        start(chunk(p, k), chunk(p, k), core_s.at[p, k], core_r.at[p, k], core_dev)

    def hop(d, p, k, i):
        j = (1 - d) // 2
        start(chunk(p, k), chunk(p, k), ring_s.at[j, i], ring_r.at[j, i], ring(d))

    for o in range(2):
        x = column(o)
        if o:
            for p in (0, 1, 5, 2, 6, 3, 7, 4):
                token_wait(x, p, x_r.at[p])
        info = meta[x, 0]
        for k in range(1, NZ):
            info = info + meta[x, k]
        ids = [jnp.concatenate([info[i : i + 1] for i in range(3 * k, 3 * k + 3)], axis=1) for k in range(2)]
        match = jnp.where(ids[0] == label, 1.0, jnp.where(ids[1] == label, 1.0, 0.0))
        rank = jnp.dot(match.astype(BF), before, preferred_element_type=F32)
        every = toks[x].reshape(cols, feat)

        def chosen(i, which):
            choose = jnp.where(rank[i : i + 1] == slot, match[i : i + 1], 0.0)
            choose = jnp.where(group == base + which, choose, 0.0).astype(BF)
            return jnp.dot(choose, every, preferred_element_type=F32).astype(BF)

        for i, (q, which) in enumerate(targets):
            pick[i, o] = chosen(i, which)
            start(pick.at[i, o], rows.at[h, c, which, x], s3.at[i, o], r3.at[i, o], (e, q))
        for k in range(2):
            rows[h, c, k, x] = chosen(len(targets), k)
            core_send(0, 2 * k + o)

    def accumulate(p, first=False):
        for k in range(4):
            arrived(rows.at[slices[p], 1 - c, tensor(p, k // 2), column(k % 2)], core_r.at[p, k])
        sl = slices[p]
        col = pl.ds(pl.multiple_of(sl * feat, 128), feat)
        x = rows[sl, :, 0].reshape(4 * PIECE, feat)
        y = rows[sl, :, 1].reshape(4 * PIECE, feat)
        for k, (lhs, w) in enumerate(((x, wg), (x, wu), (y, wd))):
            new = lax.dot_general(lhs, w[:, col], NT, preferred_element_type=F32)
            pre[k] = new if first else pre[k] + new

    def dense_part():
        for k in range(3):
            arrived(dense_w.at[k, 1 - c], dw_r.at[k])
        every = toks[...].reshape(2 * cols, feat)
        for k in range(3):
            w = dense_w[k].reshape(2 * hpad, feat)
            part = lax.dot_general(every, w, NT, preferred_element_type=F32).reshape(2, NZ, BLOCK, 2 * hpad)
            part = part[:, :, 0:TOK] if k < 2 else part[:, :, TOK:BLOCK]
            for hh in range(NH):
                part_out[hh, k] = jnp.concatenate([part[0, hh], part[1, hh]], 0).astype(BF)
        for k in range(1, NH):
            hh = lax.rem(h + k, NH)
            start(part_out.at[hh], part_in.at[k], da_s.at[k], da_r.at[k], (e, hh))

    for o in range(2):
        for k in range(2):
            arrived(chunk(4, 2 * k + o), r3.at[k, o])
            hop(1, 4, 2 * k + o, 2 * k + o)
            hop(-1, 4, 2 * k + o, 2 * k + o)
            core_send(4, 2 * k + o)
        for m, p, d in ((2, 2, -1), (3, 3, 1)):
            arrived(chunk(p, o), r3.at[m, o])
            hop(d, p, o, 6 + o)
            core_send(p, o)
        arrived(chunk(1, o), r3.at[4, o])
        hop(-1 if o else 1, 1, o, 8)
        core_send(1, o)

    dense_part()
    for load in loads:
        load.wait()
    for o in range(2):
        for k in range(2):
            for d in (1, -1):
                p = 5 if d == 1 else 6
                arrived(chunk(p, 2 * k + o), ring_r.at[(1 - d) // 2, 2 * k + o])
                if (k == 0) == (d == 1):
                    hop(d, p, 2 * k + o, 4 + o)
                core_send(p, 2 * k + o)
        if o == 0:
            accumulate(0, True)
    for o in range(2):
        for p, d in ((2, 1), (3, -1)):
            other = 5 - p
            arrived(chunk(other, 2 + o), ring_r.at[(1 - d) // 2, 6 + o])
            core_send(other, 2 + o)
        arrived(chunk(1, 2 + o), ring_r.at[o, 8])
        core_send(1, 2 + o)
    accumulate(4)
    accumulate(5)
    accumulate(6)
    for k in range(2):
        for o in range(2):
            arrived(chunk(7, 2 * k + o), ring_r.at[k, 4 + o])
            core_send(7, 2 * k + o)
        accumulate(3 - k)
    accumulate(1)
    accumulate(7)

    def dense_sum():
        sums = part_out[h].astype(F32)
        for k in range(1, NH):
            arrived(part_in.at[k], da_r.at[k])
            sums = sums + part_in[k].astype(F32)
        dense_gate, dense_up = grads_of(sums[0], sums[1], sums[2])
        dgrad[0, h] = dense_gate
        dgrad[1, h] = dense_up
        start(dgrad.at[:, h], dgrad.at[:, h], db_s.at[0], db_r.at[0], (e, plane(0, True)))
        for k in range(1, 4):
            start(dgrad.at[:, h], dgrad.at[:, h], db_s.at[k], db_r.at[k], (e, plane(k, False)))

    def dense_pass():
        ref = dgrad.at[:, plane(0, True)]
        arrived(ref, db_r.at[0])
        for k in range(1, 4):
            start(ref, ref, db_s.at[3 + k], db_r.at[3 + k], (e, plane(k, False)))

    def dense_result():
        for k in range(1, 4):
            arrived(dgrad.at[:, plane(-k, False)], db_r.at[k])
            arrived(dgrad.at[:, plane(-k, True)], db_r.at[3 + k])
        result = None
        for k in range(2):
            lhs = dgrad[k].reshape(cols, 2 * hpad)
            term = jnp.dot(lhs, dense_w[k].reshape(2 * hpad, feat), preferred_element_type=F32)
            result = term if result is None else result + term
        result = result.reshape(NZ, 2, TOK, feat)
        for x in range(2):
            res[x] = result[:, x]
        res_x_out[...] = res[1 - xl].reshape(NZ * TOK, feat).astype(BF)
        start(res_x_out, res_x_in, xx_s.at[1], xx_r.at[1], x_dev)

    def dense_reduce():
        arrived(res_x_in, xx_r.at[1])
        result = res[xl] + res_x_in[...].astype(F32).reshape(NZ, TOK, feat)
        res[xl] = result
        zero = jnp.zeros((PAD - TOK, feat), F32)
        for k in range(NZ):
            res_out[k] = jnp.concatenate([result[k], zero], 0).astype(BF)
        for k in range(1, NZ):
            start(res_out.at[at_z(k)], res_in.at[k], dz_s.at[k], dz_r.at[k], ring(k))

    new_gate, new_up = grads_of(pre[0], pre[1], pre[2])
    gg[...] = new_gate
    gu[...] = new_up

    def slot_z(i):
        odd = i % 2
        return lax.rem(z + odd * (4 - (i + 1) // 2) + (1 - odd) * (4 + i // 2), NZ)

    half = 2 * PIECE

    def produce(i):
        zd = slot_z(i)
        col = pl.ds(pl.multiple_of(lax.rem(h - zd + NH, NH) * feat, 128), feat)

        def rows_of(cc):
            sel = pl.ds(pl.multiple_of(cc * half, half), half)
            return jnp.dot(gg[sel], wg[:, col], preferred_element_type=F32) + jnp.dot(
                gu[sel], wu[:, col], preferred_element_type=F32
            )

        give[i] = rows_of(1 - c).astype(BF).reshape(2, PIECE, feat)
        start(give.at[i], got.at[i], ex_s.at[i], ex_r.at[i], core_dev)
        keep[i] = rows_of(c).reshape(2, PIECE, feat)

    cut = chain_out.shape[4]

    def settle(i):
        arrived(got.at[i], ex_r.at[i])
        keep[i] = keep[i] + got[i].astype(F32)
        side_out[i] = keep[i, 1 - xl, :, cut:feat].astype(BF)
        start(side_out.at[i], side_in.at[i], sd_s.at[i], sd_r.at[i], x_dev)

    def chain(d, step, x, i):
        k = (1 - d) // 2
        value = keep[i, x, :, 0:cut]
        if step == 1 and x == k or step > 1:
            arrived(chain_in.at[k, step - 1, x], ch_r.at[k, step - 1, x])
            value = value + chain_in[k, step - 1, x].astype(F32)
        chain_out[k, step, x] = value.astype(BF)
        start(chain_out.at[k, step, x], chain_in.at[k, step, x], ch_s.at[k, step, x], ch_r.at[k, step, x], ring(d))

    def side(i):
        arrived(side_in.at[i], sd_r.at[i])
        return keep[i, xl, :, cut:feat] + side_in[i].astype(F32)

    def side_chain(d, step, i):
        k = (1 - d) // 2
        value = side(i)
        if step > k:
            arrived(rest_in.at[k, step - 1], rs_r.at[k, step - 1])
            value = value + rest_in[k, step - 1].astype(F32)
        rest_out[k, step] = value.astype(BF)
        start(rest_out.at[k, step], rest_in.at[k, step], rs_s.at[k, step], rs_r.at[k, step], ring(d))

    dense_sum()
    produce(0)
    produce(1)
    settle(0)
    chain(1, 0, 0, 0)
    chain(-1, 0, 1, 0)
    produce(2)
    dense_pass()
    for step in range(1, 4):
        i = 2 * step - 1
        settle(i)
        if step == 1:
            chain(1, 1, 1, i)
        produce(i + 2)
        settle(i + 1)
        if step == 1:
            chain(-1, 1, 0, i + 1)
            chain(1, 1, 0, i)
            chain(-1, 1, 1, i + 1)
        else:
            for x in (1, 0):
                chain(1, step, x, i)
                chain(-1, step, 1 - x, i + 1)
        if i + 3 < 8:
            produce(i + 3)
        if step > 1:
            side_chain(-1, step - 1, i - 1)
        side_chain(1, step - 1, max(i - 2, 0))
        if step == 2:
            dense_result()
        if step == 3:
            dense_reduce()
    settle(7)
    for x in range(2):
        value = keep[7, x, :, 0:cut]
        for k in range(2):
            arrived(chain_in.at[k, 3, x], ch_r.at[k, 3, x])
            value = value + chain_in[k, 3, x].astype(F32)
        total[x] = value
    x_out[...] = total[1 - xl].astype(BF)
    start(x_out, x_in, xx_s.at[0], xx_r.at[0], x_dev)
    side_chain(-1, 3, 6)
    side_chain(1, 3, 5)
    rest = side(7)
    for k in range(2):
        arrived(rest_in.at[k, 3], rs_r.at[k, 3])
        rest = rest + rest_in[k, 3].astype(F32)
    r, t = iota((NZ * 16, PIECE), 0), iota((NZ * 16, PIECE), 1)
    spread = jnp.where(r % 16 < CAP, jnp.where(t == (r // 16) * CAP + r % 16, 1.0, 0.0), 0.0).astype(BF)
    arrived(x_in, xx_r.at[0])
    first = total[xl] + x_in[...].astype(F32)
    for lo, hi, value in ((0, cut, first), (cut, feat, rest)):
        home_out[:, :, lo:hi] = jnp.dot(spread, value.astype(BF), preferred_element_type=F32).astype(BF).reshape(NZ, 16, hi - lo)

    back = lax.rem(h - z + NH, NH)
    for k in range(1, NZ):
        zt = at_z(k)
        start(home_out.at[zt], home_in.at[k], hm_s.at[k], hm_r.at[k], dev(zt, xl, c, back))
    home = remote(home_out.at[z], home_in.at[0], hm_s.at[0], hm_r.at[0], dev(z, xl, c, back))
    stay = pltpu.make_async_copy(home_out.at[z], home_in.at[0], hm_r.at[8])

    @pl.when(z != 0)
    def _():
        home.start()

    @pl.when(z == 0)
    def _():
        stay.start()

    n = NZ * 16
    ids0, ids1 = own_ids[0][:, 0:n], own_ids[1][:, 0:n]
    gates = along(gates_ref[...])
    g0, g1 = gates[0:1, 0:n], gates[1:2, 0:n]
    r, t = iota((n, n), 0), iota((n, n), 1)
    label = ((h + (z - r // 16 + NZ) % NZ) % NH + 1).astype(F32)
    hit0, hit1 = jnp.where(ids0 == label, 1.0, 0.0), jnp.where(ids1 == label, 1.0, 0.0)
    before = jnp.where(r // TOK == t // TOK, jnp.where(r < t, 1.0, 0.0), 0.0).astype(BF)
    rank = jnp.dot((hit0 + hit1).astype(BF), before, preferred_element_type=F32)
    weigh = jnp.where(rank == (r % 16).astype(F32), hit0 * g0 + hit1 * g1, 0.0)

    dense = res[xl, z]
    for k in range(1, NZ):
        arrived(res_in.at[k], dz_r.at[k])
        dense = dense + res_in[k, 0:TOK].astype(F32)

    for k in range(1, NZ):
        arrived(home_in.at[k], hm_r.at[k])

    @pl.when(z != 0)
    def _():
        home.wait()

    @pl.when(z == 0)
    def _():
        stay.wait()

    expert = lax.dot_general(
        weigh, home_in[...].reshape(n, feat).astype(F32), (((0,), (0,)), ((), ())),
        precision=lax.Precision.HIGHEST, preferred_element_type=F32,
    )
    out_ref[...] = (cot_ref[...].astype(F32) + dense + expert[0:TOK]).astype(BF)

    for copy in sent:
        copy.wait_send()


def on_device(tokens, cotangent, route_ids, route_gates, expert_gate, expert_up, expert_down, dense_gate, dense_up, dense_down):
    feat = tokens.shape[1]
    hid, width = expert_gate.shape[1], expert_gate.shape[2]
    hpad = (hid + 15) // 16 * 16
    cut = feat // 128 * 3 // 7 * 128
    dma, vmem = pltpu.SemaphoreType.DMA, pltpu.VMEM
    scratch = [
        vmem((hid, width), BF), vmem((hid, width), BF), vmem((hid, width), BF),
        vmem((2, NZ, BLOCK, feat), BF),
        vmem((2, NZ, 8, 128), F32),
        vmem((5, 2, PIECE, feat), BF),
        vmem((NH, 2, 2, 2, PIECE, feat), BF),
        vmem((3, 4 * PIECE, hid), F32),
        vmem((4 * PIECE, hid), BF), vmem((4 * PIECE, hid), BF),
        vmem((NZ, 2, PIECE, feat), F32),
        vmem((NZ, 2, PIECE, feat), BF), vmem((NZ, 2, PIECE, feat), BF),
        vmem((2, 4, 2, PIECE, cut), BF), vmem((2, 4, 2, PIECE, cut), BF),
        vmem((NZ, PIECE, feat - cut), BF), vmem((NZ, PIECE, feat - cut), BF),
        vmem((2, 4, PIECE, feat - cut), BF), vmem((2, 4, PIECE, feat - cut), BF),
        vmem((2, PIECE, cut), F32),
        vmem((PIECE, cut), BF), vmem((PIECE, cut), BF),
        vmem((NZ, 16, feat), BF), vmem((NZ, 16, feat), BF),
        vmem((3, 2, hpad, feat), BF),
        vmem((NH, 3, BLOCK, 2 * hpad), BF), vmem((NH, 3, BLOCK, 2 * hpad), BF),
        vmem((2, NH, BLOCK, 2 * hpad), BF),
        vmem((2, NZ, TOK, feat), F32),
        vmem((NZ * TOK, feat), BF), vmem((NZ * TOK, feat), BF),
        vmem((NZ, PAD, feat), BF), vmem((NZ, PAD, feat), BF),
        dma((3,)), dma((2, 4, 4)), dma((2, 4, 4)), dma((5, 2)), dma((5, 2)),
        dma((2, 9)), dma((2, 9)), dma((8, 4)), dma((8, 4)), dma((8, 4)), dma((8, 4)),
        dma((3,)), dma((3,)), dma((8,)), dma((8,)), dma((8,)), dma((8,)), dma((8,)), dma((8,)),
        dma((8,)), dma((8,)), dma((2, 4, 2)), dma((2, 4, 2)), dma((8,)), dma((8,)), dma((2, 4)), dma((2, 4)),
        dma((2,)), dma((2,)), dma((9,)), dma((9,)),
    ]
    whole, far = pl.BlockSpec(memory_space=pltpu.VMEM), pl.BlockSpec(memory_space=pl.ANY)
    return pl.pallas_call(
        kernel,
        out_shape=jax.ShapeDtypeStruct(tokens.shape, BF),
        in_specs=[whole] * 4 + [far] * 3 + [whole] * 3,
        out_specs=whole,
        scratch_shapes=scratch,
        compiler_params=pltpu.CompilerParams(collective_id=0, has_side_effects=True, vmem_limit_bytes=56 << 20),
        name="layer",
    )(tokens, cotangent, route_ids.T, route_gates.T, expert_gate, expert_up, expert_down, dense_gate, dense_up, dense_down)


def solution(mesh):
    in_specs = (
        P("expert", "hidden"),
        P("expert", "hidden"),
        P("expert", None),
        P("expert", None),
        P("hidden", "expert", None),
        P("hidden", "expert", None),
        P("hidden", "expert", None),
        P("expert", "hidden"),
        P("expert", "hidden"),
        P("expert", "hidden"),
    )
    return jax.shard_map(on_device, mesh=mesh, in_specs=in_specs, out_specs=P("expert", "hidden"), check_vma=False)
```
